256 devices in a mesh: blk: 32 (over y_lo, z, core), grp: 8 (over x, y_hi).
Axes of the slice: x: 4, y: 4 (y_hi: 2, y_lo: 2; y = y_hi * 2 + y_lo), z: 8, core: 2. Of those that a mesh axis runs over, the one named last changes fastest.
Arguments:
- embeddings: float32 [16384, 1536], P('blk'), may hold values from -0.15 to 0.15
- partner: int32 [16384], P('blk'), may hold values from 0 to 16383, as said below
- inv_temp: int32 [1], replicated, may hold values from 8 to 20
Outputs:
- view_loss: float32 [16384], P('blk')
- grad_embed: float32 [16384, 1536], P('blk', 'grp')
The draws below stay inside these ranges and needn't reach their ends.
Inputs may be any that keep to these rules, and one draw needn't show every extreme that they name: partner[partner[i]] equals i and partner[i] differs from i for every view i.
All inputs are finite; a program needn't handle non-finite values.
Results may differ from the reference program's by a relative error of at most 0.0052.
Values may be sent and summed in bfloat16 or wider, within the bound.
A program may use at most 64 MiB of HBM per device.

```python
import jax
import jax.numpy as jnp
from jax import lax

D = 1536
ROWS = 512
VIEWS = 16384


def pair_order(key):
    return jax.random.permutation(jax.random.fold_in(key, 5), VIEWS).astype(jnp.int32)


def draw_partner(key, part):
    order = pair_order(key)
    first_half = order[0::2]
    second_half = order[1::2]
    result = jnp.zeros((VIEWS,), jnp.int32)
    return result.at[first_half].set(second_half).at[second_half].set(first_half)


def draw_embeddings(key, part):
    order = pair_order(key)
    key = jax.random.fold_in(key, 11)
    center_key, noise_key = jax.random.split(key, 2)
    rank = jnp.zeros((VIEWS,), jnp.int32).at[order].set(jnp.arange(VIEWS, dtype=jnp.int32))
    cluster_count = max(VIEWS // 64, 1)
    cluster = (rank // 2 % cluster_count).astype(jnp.int32)
    centers = jax.random.normal(center_key, (cluster_count, D), jnp.float32)
    picked = jnp.take(centers, cluster, axis=0)
    noise = jax.random.normal(noise_key, (VIEWS, D), jnp.float32)
    result = 0.025 * (0.7071 * picked + 0.7071 * noise)
    return jnp.clip(result, -0.15, 0.15)


def setup_inputs(seed: int = 0) -> dict:
    key_list = jax.random.split(jax.random.key(seed), 4)
    return {
        "embeddings": draw_embeddings(jax.random.fold_in(key_list[3], 71), 0),
        "partner": draw_partner(jax.random.fold_in(key_list[3], 71), 0),
        "inv_temp": jax.random.randint(key_list[2], (1,), 8, 21).astype(jnp.int32),
    }


def reference(embeddings, partner, inv_temp):
    temper = inv_temp[0].astype(jnp.float32)
    total_views = embeddings.shape[0]
    rinv = lax.rsqrt(lax.optimization_barrier(jnp.sum(embeddings * embeddings, axis=1, keepdims=True)) + 1e-06)
    unit = embeddings * rinv
    query = unit.astype(jnp.bfloat16)
    col_ids = jnp.arange(total_views, dtype=jnp.int32)
    block_count = total_views // ROWS

    def block_scores(index):
        first_row = (index * ROWS).astype(jnp.int32)
        rows_q = lax.dynamic_slice_in_dim(query, first_row, ROWS, 0)
        mates = lax.dynamic_slice_in_dim(partner, first_row, ROWS, 0)
        scores = temper * lax.dot_general(rows_q, query, (((1,), (1,)), ((), ())), preferred_element_type=jnp.float32)
        row_ids = first_row + jnp.arange(ROWS, dtype=jnp.int32)
        expon = jnp.where(row_ids[:, None] != col_ids[None, :], jnp.exp(scores - temper), 0.0)
        is_mate = mates[:, None] == col_ids[None, :]
        return (scores, expon, is_mate, first_row)

    def first_pass(index):
        scores, expon, is_mate, first_row = block_scores(index)
        return (lax.optimization_barrier(jnp.sum(expon, axis=1)), lax.optimization_barrier(jnp.sum(jnp.where(is_mate, scores, 0.0), axis=1)))
    sums, pos = lax.map(first_pass, jnp.arange(block_count, dtype=jnp.int32))
    sums = sums.reshape(total_views)
    pos = pos.reshape(total_views)
    view_loss = temper + jnp.log(sums) - pos
    inverse = 1.0 / sums

    def second_pass(index):
        scores, expon, is_mate, first_row = block_scores(index)
        row_inv = lax.dynamic_slice_in_dim(inverse, first_row, ROWS, 0)
        weights = expon * (row_inv[:, None] + inverse[None, :]) - jnp.where(is_mate, 2.0, 0.0)
        return jnp.dot(weights.astype(jnp.bfloat16), query, preferred_element_type=jnp.float32)
    summed = lax.map(second_pass, jnp.arange(block_count, dtype=jnp.int32)).reshape(total_views, embeddings.shape[1])
    grad_unit = temper * summed
    inner = lax.optimization_barrier(jnp.sum(unit * grad_unit, axis=1, keepdims=True))
    grad_embed = (grad_unit - unit * inner) * rinv
    return (view_loss, grad_embed)
```

```python
import functools

import jax
import jax.numpy as jnp
from jax import lax
from jax.experimental import pallas as pl
from jax.experimental.pallas import tpu as pltpu
from jax.sharding import PartitionSpec as P

MESH = pl.DeviceIdType.MESH
ROWS = 512
FEATS = 1536
SEG = 32
CHUNK = 256
KEYS = 2048
QUART = 384
HALF = 256


def slot(dist, side, other_y, other_core, part):
    if dist in (0, 4):
        return (0 if dist == 0 else 7 * CHUNK) + 128 * other_y + 64 * other_core + 32 * part
    return (2 * dist - 1 + other_y) * CHUNK + 128 * other_core + 64 * side + 32 * part


def kernel(
    temp_ref, partner_ref, emb_hbm, loss_ref, grad_ref,
    emb, query, rinv, keys, scores, expon, weights, sum_acc, pos_acc, row_inv, mate_col,
    stat_out, stat_in, inv_in, inv_sib, far_buf, near_buf, hold_top, hold_bot, relay_in, side_in, acc, cross_out, cross_in,
    load_sem, ag_send, ag_recv, stat_sem, inv_sem, rs_send, rs_recv,
):
    blk = lax.axis_index("blk")
    grp = lax.axis_index("grp")
    ylo = lax.div(blk, 16)
    z = lax.rem(lax.div(blk, 2), 8)
    core = lax.rem(blk, 2)
    x = lax.div(grp, 2)
    yhi = lax.rem(grp, 2)
    y = yhi * 2 + ylo
    part_a = yhi
    part_b = lax.rem(yhi + ylo, 2)

    def device(x_, y_, z_, core_):
        return (lax.rem(y_, 2) * 16 + z_ * 2 + core_, x_ * 2 + lax.div(y_, 2))

    z_right = device(x, y, lax.rem(z + 1, 8), core)
    z_left = device(x, y, lax.rem(z + 7, 8), core)
    y_a = y + 1 - 2 * ylo
    y_b = 3 - y
    dev_a = device(x, y_a, z, core)
    dev_b = device(x, y_b, z, core)
    sib = device(x, y, z, 1 - core)
    x_right = device(lax.rem(x + 1, 4), y, z, core)
    x_left = device(lax.rem(x + 3, 4), y, z, core)
    dev_cross = device(x, lax.rem(y + 2, 4), z, core)
    peers = [(blk, lax.rem(grp + r, 8)) for r in range(1, 8)]

    loads = []
    for i in range(4):
        rows = pl.ds(pl.multiple_of(lax.rem(x + i, 4) * 128, 128), 128)
        copy = pltpu.make_async_copy(emb_hbm.at[rows], emb.at[rows], load_sem.at[i])
        copy.start()
        loads.append(copy)

    barrier = pltpu.get_barrier_semaphore()
    greeted = [z_right, z_left, dev_a, dev_b, sib] + peers
    for target in greeted:
        pl.semaphore_signal(barrier, inc=1, device_id=target, device_id_type=MESH)

    temper = temp_ref[0].astype(jnp.float32)

    def normalize(i):
        loads[i].wait()
        first = lax.rem(x + i, 4) * 128

        def step(j, carry):
            rows = pl.ds(pl.multiple_of(first + j * 32, 32), 32)
            e = emb[rows, :]
            r = lax.rsqrt(jnp.sum(e * e, axis=1, keepdims=True) + 1e-06)
            query[rows, :] = (e * r).astype(jnp.bfloat16)
            rinv[rows, :] = jnp.broadcast_to(r, (32, 128))
            return carry

        lax.fori_loop(0, 4, step, 0)

    normalize(0)
    rows_a = pl.ds(pl.multiple_of(x * 128 + part_a * 32, 32), SEG)
    rows_b = pl.ds(pl.multiple_of(x * 128 + 64 + part_b * 32, 32), SEG)
    keys[0:SEG, :] = query[rows_a, :]
    keys[SEG : 2 * SEG, :] = query[rows_b, :]

    pl.semaphore_wait(barrier, len(greeted))

    messages = []

    def message(src, dst, rows, target):
        i = len(messages)
        copy = pltpu.make_async_remote_copy(
            src_ref=keys.at[pl.ds(src, rows)],
            dst_ref=keys.at[pl.ds(dst, rows)],
            send_sem=ag_send.at[i],
            recv_sem=ag_recv.at[i],
            device_id=target,
            device_id_type=MESH,
        )
        messages.append(copy)
        return copy

    ring, across, twin = {}, {}, {}
    for dist in range(1, 5):
        for part in (0, 1):
            for side in (0, 1):
                if dist == 4 and side != part:
                    continue
                src = slot(dist - 1, side, 0, 0, part)
                dst = slot(dist, side, 0, 0, part)
                ring[side, dist, part] = message(src, dst, SEG, z_right if side == 0 else z_left)
    for dist in range(5):
        for side in (0, 1):
            if dist in (0, 4) and side == 1:
                continue
            for part in (0, 1):
                across[side, dist, part] = message(
                    slot(dist, side, 0, 0, part), slot(dist, side, 1, 0, part), SEG, dev_a if part == 0 else dev_b
                )
            for other in (0, 1):
                twin[side, dist, other] = message(
                    slot(dist, side, other, 0, 0), slot(dist, side, other, 1, 0), 2 * SEG, sib
                )

    lane = lax.broadcasted_iota(jnp.int32, (1, CHUNK), 1)

    def key_ids(chunk):
        if chunk in (0, 7):
            zk = lax.rem(z + (0 if chunk == 0 else 4), 8)
            yk = jnp.where(lane < 128, ylo, 1 - ylo)
            ck = jnp.where(lane % 128 < 64, core, 1 - core)
        else:
            dist = (chunk + 1) // 2
            zk = jnp.where(lane % 128 < 64, lax.rem(z + 8 - dist, 8), lax.rem(z + dist, 8))
            yk = ylo if chunk % 2 == 1 else 1 - ylo
            ck = jnp.where(lane < 128, core, 1 - core)
        within = jnp.where(lane % 64 < 32, part_a * 32, part_b * 32 + 64) + lane % 32
        return (((yk * 8 + zk) * 2 + ck) * ROWS + x * 128 + within).astype(jnp.float32)

    def score_chunk(chunk):
        cols = slice(chunk * CHUNK, (chunk + 1) * CHUNK)
        ids = key_ids(chunk)

        def step(j, carry):
            rows = pl.ds(pl.multiple_of(j * HALF, HALF), HALF)
            s = temper * lax.dot_general(
                query[rows, :], keys[cols, :], (((1,), (1,)), ((), ())), preferred_element_type=jnp.float32
            )
            e = jnp.exp(s - temper)
            if chunk == 0:
                own = lax.broadcasted_iota(jnp.int32, (HALF, CHUNK), 0) + (blk * ROWS + j * HALF)
                e = jnp.where(own.astype(jnp.float32) == ids, 0.0, e)
            mate = mate_col[rows, :]
            mate = jnp.concatenate([mate, mate], axis=1)
            p = jnp.where(mate == ids, s, 0.0)
            scores[rows, cols] = s
            expon[rows, cols] = e
            if chunk == 0:
                sum_acc[rows, :] = e[:, :128] + e[:, 128:]
                pos_acc[rows, :] = p[:, :128] + p[:, 128:]
            else:
                sum_acc[rows, :] += e[:, :128] + e[:, 128:]
                pos_acc[rows, :] += p[:, :128] + p[:, 128:]
            return carry

        lax.fori_loop(0, ROWS // HALF, step, 0)

    for part in (0, 1):
        for side in (0, 1):
            ring[side, 1, part].start()
    for part in (0, 1):
        across[0, 0, part].start()
    twin[0, 0, 0].start()
    mate_row = jnp.broadcast_to(partner_ref[...].astype(jnp.float32), (128, ROWS))
    mate_col[...] = mate_row.T
    for i in range(1, 4):
        normalize(i)

    def finish_across(dist):
        for side in ((0,) if dist in (0, 4) else (0, 1)):
            for part in (0, 1):
                across[side, dist, part].wait_recv()
            twin[side, dist, 1].start()

    def finish_twin(dist, other):
        for side in ((0,) if dist in (0, 4) else (0, 1)):
            twin[side, dist, other].wait_recv()

    for dist in range(1, 4):
        for part in (0, 1):
            for side in (0, 1):
                ring[side, dist, part].wait_recv()
                if dist < 3 or side == part:
                    ring[side, dist + 1, part].start()
                across[side, dist, part].start()
                if part == 1:
                    twin[side, dist, 0].start()
            if part == 0:
                finish_across(dist - 1)
                if dist > 1:
                    finish_twin(dist - 1, 0)
                    score_chunk(2 * (dist - 1) - 1)
            else:
                finish_twin(dist - 1, 1)
                if dist == 1:
                    finish_twin(0, 0)
                    score_chunk(0)
                else:
                    score_chunk(2 * (dist - 1))
    for part in (0, 1):
        ring[part, 4, part].wait_recv()
        across[0, 4, part].start()
    twin[0, 4, 0].start()
    finish_across(3)
    finish_twin(3, 0)
    score_chunk(5)
    finish_twin(3, 1)
    score_chunk(6)
    finish_across(4)
    finish_twin(4, 0)
    finish_twin(4, 1)
    score_chunk(7)

    stat_out[0:1, :] = jnp.sum(sum_acc[...].T, axis=0, keepdims=True)
    stat_out[1:2, :] = jnp.sum(pos_acc[...].T, axis=0, keepdims=True)
    for r in range(1, 8):
        pltpu.make_async_remote_copy(
            src_ref=stat_out,
            dst_ref=stat_in.at[r],
            send_sem=stat_sem.at[0],
            recv_sem=stat_sem.at[1],
            device_id=peers[r - 1],
            device_id_type=MESH,
        ).start()
    for copy in messages:
        copy.wait_send()
    stat_all = pltpu.make_async_remote_copy(
        src_ref=stat_in.at[pl.ds(1, 7)],
        dst_ref=stat_in.at[pl.ds(1, 7)],
        send_sem=stat_sem.at[0],
        recv_sem=stat_sem.at[1],
        device_id=peers[0],
        device_id_type=MESH,
    )
    stat_all.wait_recv()
    total = stat_out[...]
    for r in range(1, 8):
        total = total + stat_in[r]
    sums = total[0:1, :]
    inverse = 1.0 / sums
    loss_ref[...] = temper + jnp.log(sums) - total[1:2, :]

    row_inv[0:128, :] = jnp.broadcast_to(inverse[:, 0:128], (128, 128)).T
    row_inv[128:256, :] = jnp.broadcast_to(inverse[:, 128:256], (128, 128)).T
    row_inv[256:384, :] = jnp.broadcast_to(inverse[:, 256:384], (128, 128)).T
    row_inv[384:512, :] = jnp.broadcast_to(inverse[:, 384:512], (128, 128)).T
    tile = jnp.where(x == 0, inverse[:, 0:128], inverse[:, 128:256])
    tile = jnp.where(x == 2, inverse[:, 256:384], tile)
    tile = jnp.where(x == 3, inverse[:, 384:512], tile)
    lane1 = lax.broadcasted_iota(jnp.int32, (1, 128), 1)
    by32 = jnp.concatenate([tile[:, 32:], tile[:, :32]], axis=1)
    by64 = jnp.concatenate([tile[:, 64:], tile[:, :64]], axis=1)
    first = jnp.where(part_a == 0, tile, by32)
    second = jnp.where(part_b == 0, by32, by64)
    pair = jnp.where(lane1 < 32, first, second)
    pair = jnp.where(lane1 < 64, pair, jnp.concatenate([pair[:, 64:], pair[:, :64]], axis=1))
    inv_in[0] = pair
    inv_targets = [(dz, device(x, y, lax.rem(z + dz, 8), core)) for dz in range(1, 8)]
    inv_targets += [(8 + dz, device(x, y_a, lax.rem(z + dz, 8), core)) for dz in range(8)]
    inv_targets += [(16 + dz, device(x, y_b, lax.rem(z + dz, 8), core)) for dz in range(8)]
    for i, target in inv_targets:
        pltpu.make_async_remote_copy(
            src_ref=inv_in.at[0],
            dst_ref=inv_in.at[i],
            send_sem=inv_sem.at[0],
            recv_sem=inv_sem.at[1],
            device_id=target,
            device_id_type=MESH,
        ).start()
    stat_all.wait_send()
    inv_all = pltpu.make_async_remote_copy(
        src_ref=inv_in.at[pl.ds(1, 23)],
        dst_ref=inv_in.at[pl.ds(1, 23)],
        send_sem=inv_sem.at[0],
        recv_sem=inv_sem.at[1],
        device_id=sib,
        device_id_type=MESH,
    )
    inv_all.wait_recv()
    inv_twin = pltpu.make_async_remote_copy(
        src_ref=inv_in,
        dst_ref=inv_sib,
        send_sem=inv_sem.at[2],
        recv_sem=inv_sem.at[3],
        device_id=sib,
        device_id_type=MESH,
    )
    inv_twin.start()
    inv_twin.wait_recv()

    def key_inv(chunk):
        low = lane1 < 64
        is_a = lane1 % 64 < 32

        def of(ref, dz, other_y):
            if other_y == 0:
                return ref[dz]
            return jnp.where(is_a, ref[8 + dz], ref[16 + dz])

        if chunk in (0, 7):
            dz = 0 if chunk == 0 else 4
            tiles = [jnp.where(low, of(inv_in, dz, o), of(inv_sib, dz, o)) for o in (0, 1)]
        else:
            dist = (chunk + 1) // 2
            o = 0 if chunk % 2 == 1 else 1
            tiles = [jnp.where(low, of(ref, dist, o), of(ref, 8 - dist, o)) for ref in (inv_in, inv_sib)]
        return jnp.concatenate(tiles, axis=1)

    for chunk in range(8):
        cols = slice(chunk * CHUNK, (chunk + 1) * CHUNK)
        ids = key_ids(chunk)
        col_inv = key_inv(chunk)

        def weigh(j, carry, cols=cols, ids=ids, col_inv=col_inv, chunk=chunk):
            rows = pl.ds(pl.multiple_of(j * 64, 64), 64)
            ri = row_inv[rows, :]
            mate = mate_col[rows, :]
            w = expon[rows, cols] * (jnp.concatenate([ri, ri], axis=1) + col_inv)
            w = w - jnp.where(jnp.concatenate([mate, mate], axis=1) == ids, 2.0, 0.0)
            w = w.astype(jnp.bfloat16)
            weights[rows, cols] = w
            inner = w.astype(jnp.float32) * scores[rows, cols]
            inner = inner[:, :128] + inner[:, 128:]
            if chunk == 0:
                sum_acc[rows, :] = inner
            else:
                sum_acc[rows, :] += inner
            return carry

        lax.fori_loop(0, ROWS // 64, weigh, 0)

    def coefs(j, carry):
        rows = pl.ds(pl.multiple_of(j * 64, 64), 64)
        r = rinv[rows, :]
        inner = jnp.sum(sum_acc[rows, :], axis=1, keepdims=True)
        pos_acc[rows, :] = r * r * inner
        sum_acc[rows, :] = r * temper
        return carry

    lax.fori_loop(0, ROWS // 64, coefs, 0)

    def grad_piece(ahead, top):
        cols = pl.ds(pl.multiple_of(lax.rem(x + ahead, 4) * QUART, QUART), QUART)
        rows = pl.ds(0 if top else HALF, HALF)
        d = jnp.dot(weights[rows, :], keys[:, cols], preferred_element_type=jnp.float32)
        u = sum_acc[rows, :]
        v = pos_acc[rows, :]
        return d * jnp.concatenate([u] * 3, axis=1) - emb[rows, cols] * jnp.concatenate([v] * 3, axis=1)

    def rs_message(i, src, dst, target):
        return pltpu.make_async_remote_copy(
            src_ref=src, dst_ref=dst, send_sem=rs_send.at[i], recv_sem=rs_recv.at[i],
            device_id=target, device_id_type=MESH,
        )

    far_right = rs_message(0, far_buf.at[0], relay_in.at[0], x_right)
    far_left = rs_message(1, far_buf.at[1], relay_in.at[1], x_left)
    right_bot = rs_message(2, near_buf.at[0], side_in.at[0], x_right)
    left_top = rs_message(3, near_buf.at[1], side_in.at[1], x_left)
    right_top = rs_message(4, near_buf.at[2], side_in.at[2], x_right)
    left_bot = rs_message(5, near_buf.at[3], side_in.at[3], x_left)
    cross = rs_message(6, cross_out, cross_in, dev_cross)

    far_buf[0] = grad_piece(2, True).astype(jnp.bfloat16)
    far_right.start()
    far_buf[1] = grad_piece(2, False).astype(jnp.bfloat16)
    far_left.start()
    near_buf[0] = grad_piece(1, False).astype(jnp.bfloat16)
    right_bot.start()
    near_buf[1] = grad_piece(3, True).astype(jnp.bfloat16)
    left_top.start()
    hold_top[...] = grad_piece(1, True)
    hold_bot[...] = grad_piece(3, False)
    far_right.wait_recv()
    near_buf[2] = (hold_top[...] + relay_in[0].astype(jnp.float32)).astype(jnp.bfloat16)
    right_top.start()
    far_left.wait_recv()
    near_buf[3] = (hold_bot[...] + relay_in[1].astype(jnp.float32)).astype(jnp.bfloat16)
    left_bot.start()
    acc[0:HALF, :] = grad_piece(0, True)
    acc[HALF:ROWS, :] = grad_piece(0, False)
    right_bot.wait_recv()
    left_top.wait_recv()
    acc[HALF:ROWS, :] += side_in[0].astype(jnp.float32)
    acc[0:HALF, :] += side_in[1].astype(jnp.float32)
    right_top.wait_recv()
    left_bot.wait_recv()
    acc[0:HALF, :] += side_in[2].astype(jnp.float32)
    acc[HALF:ROWS, :] += side_in[3].astype(jnp.float32)
    whole = acc[...]
    first_half, second_half = whole[:, :192], whole[:, 192:]
    cross_out[...] = jnp.where(yhi == 0, second_half, first_half).astype(jnp.bfloat16)
    cross.start()
    grad_ref[...] = jnp.where(yhi == 0, first_half, second_half)
    cross.wait_recv()
    grad_ref[...] += cross_in[...].astype(jnp.float32)
    inv_all.wait_send()
    inv_twin.wait_send()
    for copy in (far_right, far_left, right_bot, left_top, right_top, left_bot, cross):
        copy.wait_send()


def shards(embeddings, partner, inv_temp):
    f32, bf16 = jnp.float32, jnp.bfloat16
    vmem = pl.BlockSpec(memory_space=pltpu.VMEM)
    loss, grad = pl.pallas_call(
        kernel,
        out_shape=(jax.ShapeDtypeStruct((1, ROWS), f32), jax.ShapeDtypeStruct((ROWS, 192), f32)),
        in_specs=[pl.BlockSpec(memory_space=pltpu.SMEM), vmem, pl.BlockSpec(memory_space=pl.ANY)],
        out_specs=(vmem, vmem),
        scratch_shapes=[
            pltpu.VMEM((ROWS, FEATS), f32),
            pltpu.VMEM((ROWS, FEATS), bf16),
            pltpu.VMEM((ROWS, 128), f32),
            pltpu.VMEM((KEYS, FEATS), bf16),
            pltpu.VMEM((ROWS, KEYS), f32),
            pltpu.VMEM((ROWS, KEYS), f32),
            pltpu.VMEM((ROWS, KEYS), bf16),
            pltpu.VMEM((ROWS, 128), f32),
            pltpu.VMEM((ROWS, 128), f32),
            pltpu.VMEM((ROWS, 128), f32),
            pltpu.VMEM((ROWS, 128), f32),
            pltpu.VMEM((2, ROWS), f32),
            pltpu.VMEM((8, 2, ROWS), f32),
            pltpu.VMEM((24, 1, 128), f32),
            pltpu.VMEM((24, 1, 128), f32),
            pltpu.VMEM((2, HALF, QUART), bf16),
            pltpu.VMEM((4, HALF, QUART), bf16),
            pltpu.VMEM((HALF, QUART), f32),
            pltpu.VMEM((HALF, QUART), f32),
            pltpu.VMEM((2, HALF, QUART), bf16),
            pltpu.VMEM((4, HALF, QUART), bf16),
            pltpu.VMEM((ROWS, QUART), f32),
            pltpu.VMEM((ROWS, 192), bf16),
            pltpu.VMEM((ROWS, 192), bf16),
            pltpu.SemaphoreType.DMA((4,)),
            pltpu.SemaphoreType.DMA((48,)),
            pltpu.SemaphoreType.DMA((48,)),
            pltpu.SemaphoreType.DMA((2,)),
            pltpu.SemaphoreType.DMA((4,)),
            pltpu.SemaphoreType.DMA((7,)),
            pltpu.SemaphoreType.DMA((7,)),
        ],
        compiler_params=pltpu.CompilerParams(
            collective_id=0, has_side_effects=True, vmem_limit_bytes=48 * 1024 * 1024
        ),
    )(inv_temp, partner.reshape(1, ROWS), embeddings)
    return (loss.reshape(ROWS), grad)


def solution(mesh):
    in_specs = (P("blk", None), P("blk"), P())
    out_specs = (P("blk"), P("blk", "grp"))
    return jax.shard_map(shards, mesh=mesh, in_specs=in_specs, out_specs=out_specs, check_vma=False)
```

```python
import jax
import jax.numpy as jnp
from jax import lax
from jax.experimental import pallas as pl
from jax.experimental.pallas import tpu as pltpu
from jax.sharding import PartitionSpec as P

MESH = pl.DeviceIdType.MESH
ROWS = 512
FEATS = 1536
SUB = 16
CHUNK = 256
KEYS = 2048
QUART = 384
HALF = 256
FORTH = 128


def tile_of(dist, side, other_y):
    if dist in (0, 4):
        return (0 if dist == 0 else 14) + other_y
    return 2 * (2 * dist - 1 + other_y) + side


TILES = {}
for _d in range(5):
    for _s in (0, 1):
        for _o in (0, 1):
            if not (_d in (0, 4) and _s == 1):
                TILES[tile_of(_d, _s, _o)] = (_d, _s, _o)


def slot(dist, side, other_y, other_core, piece):
    return 128 * tile_of(dist, side, other_y) + 64 * other_core + SUB * piece


def turn(v):
    return pltpu.roll(v, 64, axis=1)


def pack(v, mask):
    n = v.shape[0] // 2
    return jnp.where(mask, v[:n], turn(v[n:]))


def unpack(m):
    return jnp.concatenate([m, turn(m)], axis=0)


def kernel(
    temp_ref, partner_ref, emb_hbm, loss_ref, grad_ref,
    emb, query, rinv, keys, scores, expon, weights, sum_acc, pos_acc, row_inv, mate_col,
    stat_out, stat_in, col_out, col_near, col_sum, col_far, key_tot,
    far_buf, near_buf, relay_in, side_in, hold_x, acc, hold_full, hold_half,
    yo_buf, yi_buf, cross_out, cross_in, xo_buf, xi_buf,
    load_sem, ag_send, ag_recv, stat_sem, col_sem, rs_send, rs_recv,
):
    blk = lax.axis_index("blk")
    grp = lax.axis_index("grp")
    ylo = lax.div(blk, 16)
    z = lax.rem(lax.div(blk, 2), 8)
    core = lax.rem(blk, 2)
    x = lax.div(grp, 2)
    yhi = lax.rem(grp, 2)
    y = yhi * 2 + ylo
    part_a = yhi
    part_b = lax.rem(yhi + ylo, 2)

    def device(x_, y_, z_, core_):
        return (lax.rem(y_, 2) * 16 + z_ * 2 + core_, x_ * 2 + lax.div(y_, 2))

    z_right = device(x, y, lax.rem(z + 1, 8), core)
    z_left = device(x, y, lax.rem(z + 7, 8), core)
    y_a = y + 1 - 2 * ylo
    y_b = 3 - y
    dev_a = device(x, y_a, z, core)
    dev_b = device(x, y_b, z, core)
    sib = device(x, y, z, 1 - core)
    x_right = device(lax.rem(x + 1, 4), y, z, core)
    x_left = device(lax.rem(x + 3, 4), y, z, core)
    x_far = device(lax.rem(x + 2, 4), y, z, core)
    dev_cross = device(x, lax.rem(y + 2, 4), z, core)
    peers = [(blk, lax.rem(grp + r, 8)) for r in range(1, 8)]

    barrier = pltpu.get_barrier_semaphore()
    greeted = [z_right, z_left, dev_a, dev_b, sib] + peers
    for target in greeted:
        pl.semaphore_signal(barrier, inc=1, device_id=target, device_id_type=MESH)

    loads = []
    for i in range(4):
        rows = pl.ds(pl.multiple_of(lax.rem(x + i, 4) * 128, 128), 128)
        copy = pltpu.make_async_copy(emb_hbm.at[rows], emb.at[rows], load_sem.at[i])
        copy.start()
        loads.append(copy)

    temper = temp_ref[0].astype(jnp.float32)

    def unit_rows(rows):
        e = emb[rows, :]
        r = lax.rsqrt(jnp.sum(e * e, axis=1, keepdims=True) + 1e-06)
        return (e * r).astype(jnp.bfloat16), r

    def normalize(i):
        first = lax.rem(x + i, 4) * 128

        def step(j, carry):
            for k in range(4):
                rows = pl.ds(pl.multiple_of(first + j * 64 + k * SUB, SUB), SUB)
                q, r = unit_rows(rows)
                query[rows, :] = q
                rinv[rows, :] = jnp.broadcast_to(r, (SUB, 128))
            return carry

        lax.fori_loop(0, 2, step, 0)

    loads[0].wait()
    for piece in range(4):
        first = x * 128 + (part_a * 32 if piece < 2 else 64 + part_b * 32) + SUB * (piece % 2)
        q, _ = unit_rows(pl.ds(pl.multiple_of(first, SUB), SUB))
        keys[SUB * piece : SUB * (piece + 1), :] = q

    pl.semaphore_wait(barrier, len(greeted))

    messages = []

    def message(src, dst, rows, target):
        i = len(messages)
        copy = pltpu.make_async_remote_copy(
            src_ref=keys.at[pl.ds(src, rows)],
            dst_ref=keys.at[pl.ds(dst, rows)],
            send_sem=ag_send.at[i],
            recv_sem=ag_recv.at[i],
            device_id=target,
            device_id_type=MESH,
        )
        messages.append(copy)
        return copy

    ring, across, twin = {}, {}, {}
    for dist in range(1, 5):
        for piece in range(4):
            for side in (0, 1):
                if dist == 4 and side != piece // 2:
                    continue
                src = slot(dist - 1, 0 if dist == 1 else side, 0, 0, piece)
                dst = slot(dist, 0 if dist == 4 else side, 0, 0, piece)
                ring[side, dist, piece] = message(src, dst, SUB, z_right if side == 0 else z_left)
    for dist in range(5):
        for side in (0, 1):
            if dist in (0, 4) and side == 1:
                continue
            for piece in range(4):
                across[side, dist, piece] = message(
                    slot(dist, side, 0, 0, piece), slot(dist, side, 1, 0, piece), SUB, dev_a if piece < 2 else dev_b
                )
            for other in (0, 1):
                twin[side, dist, other] = message(
                    slot(dist, side, other, 0, 0), slot(dist, side, other, 1, 0), 4 * SUB, sib
                )

    lane = lax.broadcasted_iota(jnp.int32, (1, 128), 1)

    def tile_place(tile):
        dist, side, other = TILES[tile]
        return lax.rem(z + (8 - dist if side == 0 else dist), 8), other

    def key_ids(chunk):
        ids = []
        for tile in (2 * chunk, 2 * chunk + 1):
            zk, other = tile_place(tile)
            yk = ylo if other == 0 else 1 - ylo
            ck = jnp.where(lane < 64, core, 1 - core)
            within = jnp.where(lane % 64 < 32, part_a * 32, part_b * 32 + 64) + lane % 32
            ids.append((((yk * 8 + zk) * 2 + ck) * ROWS + x * 128 + within).astype(jnp.float32))
        return jnp.concatenate(ids, axis=1)

    def score_chunk(chunk):
        cols = slice(chunk * CHUNK, (chunk + 1) * CHUNK)
        ids = key_ids(chunk)

        def step(j, carry):
            rows = pl.ds(pl.multiple_of(j * HALF, HALF), HALF)
            s = temper * lax.dot_general(
                query[rows, :], keys[cols, :], (((1,), (1,)), ((), ())), preferred_element_type=jnp.float32
            )
            e = jnp.exp(s - temper)
            if chunk == 0:
                own = lax.broadcasted_iota(jnp.int32, (HALF, CHUNK), 0) + (blk * ROWS + j * HALF)
                e = jnp.where(own.astype(jnp.float32) == ids, 0.0, e)
            mate = mate_col[rows, :]
            mate = jnp.concatenate([mate, mate], axis=1)
            p = jnp.where(mate == ids, s, 0.0)
            scores[rows, cols] = s
            expon[rows, cols] = e
            if chunk == 0:
                sum_acc[rows, :] = e[:, :128] + e[:, 128:]
                pos_acc[rows, :] = p[:, :128] + p[:, 128:]
            else:
                sum_acc[rows, :] += e[:, :128] + e[:, 128:]
                pos_acc[rows, :] += p[:, :128] + p[:, 128:]
            return carry + jnp.sum(e, axis=0, keepdims=True)

        total = lax.fori_loop(0, ROWS // HALF, step, jnp.zeros((1, CHUNK), jnp.float32))
        for i in (0, 1):
            zk, other = tile_place(2 * chunk + i)
            col_out[pl.ds(other * 8 + zk, 1), :] = total[:, 128 * i : 128 * (i + 1)]

    for piece in range(4):
        for side in (0, 1):
            ring[side, 1, piece].start()
        across[0, 0, piece].start()
    twin[0, 0, 0].start()
    normalize(0)
    loads[1].wait()
    normalize(1)

    def sides(dist):
        return (0,) if dist in (0, 4) else (0, 1)

    def finish_across(dist):
        for side in sides(dist):
            for piece in range(4):
                across[side, dist, piece].wait_recv()
            twin[side, dist, 1].start()

    def finish_twin(dist, other):
        for side in sides(dist):
            twin[side, dist, other].wait_recv()

    for dist in range(1, 4):
        for piece in range(4):
            for side in (0, 1):
                ring[side, dist, piece].wait_recv()
                if dist < 3 or side == piece // 2:
                    ring[side, dist + 1, piece].start()
                across[side, dist, piece].start()
                if piece == 3:
                    twin[side, dist, 0].start()
            if dist == 1:
                if piece == 0:
                    loads[2].wait()
                    normalize(2)
                elif piece == 1:
                    loads[3].wait()
                    normalize(3)
                    mate_row = jnp.broadcast_to(partner_ref[...].astype(jnp.float32), (128, ROWS))
                    mate_col[...] = mate_row.T
                elif piece == 2:
                    finish_across(0)
                else:
                    finish_twin(0, 0)
                    finish_twin(0, 1)
                    score_chunk(0)
            else:
                if piece == 0:
                    finish_twin(dist - 1, 0)
                    score_chunk(2 * (dist - 1) - 1)
                elif piece == 1:
                    finish_across(dist - 1)
                elif piece == 2:
                    finish_twin(dist - 1, 1)
                    score_chunk(2 * (dist - 1))
    for piece in (0, 2, 1, 3):
        ring[piece // 2, 4, piece].wait_recv()
        across[0, 4, piece].start()
    twin[0, 4, 0].start()
    finish_twin(3, 0)
    score_chunk(5)
    finish_across(3)
    finish_twin(3, 1)
    score_chunk(6)
    finish_across(4)
    finish_twin(4, 0)
    finish_twin(4, 1)
    score_chunk(7)

    def small(src, dst, sems, i, target):
        return pltpu.make_async_remote_copy(
            src_ref=src, dst_ref=dst, send_sem=sems.at[i], recv_sem=sems.at[i + 1],
            device_id=target, device_id_type=MESH,
        )

    near_targets = [sib, dev_a, dev_b, device(x, y_a, z, 1 - core), device(x, y_b, z, 1 - core)]
    for i, target in enumerate(near_targets):
        small(col_out, col_near.at[i], col_sem, 0, target).start()
    stat_out[0:1, :] = jnp.sum(sum_acc[...].T, axis=0, keepdims=True)
    stat_out[1:2, :] = jnp.sum(pos_acc[...].T, axis=0, keepdims=True)
    for r in range(1, 8):
        small(stat_out, stat_in.at[r], stat_sem, 0, peers[r - 1]).start()
    near_all = small(col_near, col_near, col_sem, 0, sib)
    near_all.wait_recv()
    is_a = lax.broadcasted_iota(jnp.int32, (16, 128), 1) % 64 < 32

    def flip(v):
        return jnp.concatenate([v[8:], v[:8]], axis=0)

    over_a = flip(col_near[1] + turn(col_near[3]))
    over_b = flip(col_near[2] + turn(col_near[4]))
    col_sum[...] = col_out[...] + turn(col_near[0]) + jnp.where(is_a, over_a, over_b)
    for dz in range(1, 8):
        small(col_sum, col_far.at[dz], col_sem, 2, device(x, y, lax.rem(z + dz, 8), core)).start()
    for copy in messages:
        copy.wait_send()
    stat_all = small(stat_in.at[pl.ds(1, 7)], stat_in.at[pl.ds(1, 7)], stat_sem, 0, peers[0])
    stat_all.wait_recv()
    total = stat_out[...]
    for r in range(1, 8):
        total = total + stat_in[r]
    sums = total[0:1, :]
    inverse = 1.0 / sums
    loss_ref[...] = temper + jnp.log(sums) - total[1:2, :]
    for i in range(4):
        part = slice(128 * i, 128 * (i + 1))
        row_inv[part, :] = jnp.broadcast_to(inverse[:, part], (128, 128)).T
    far_all = small(col_far.at[pl.ds(1, 7)], col_far.at[pl.ds(1, 7)], col_sem, 2, z_right)
    far_all.wait_recv()
    col_total = col_sum[...]
    for dz in range(1, 8):
        col_total = col_total + col_far[dz]
    key_tot[...] = 1.0 / col_total

    def weigh_rows(first):
        for chunk in range(8):
            cols = slice(chunk * CHUNK, (chunk + 1) * CHUNK)
            ids = key_ids(chunk)
            inv = []
            for tile in (2 * chunk, 2 * chunk + 1):
                zk, other = tile_place(tile)
                inv.append(key_tot[pl.ds(other * 8 + zk, 1), :])
            col_inv = jnp.concatenate(inv, axis=1)

            def weigh(j, carry, cols=cols, ids=ids, col_inv=col_inv, chunk=chunk):
                rows = pl.ds(pl.multiple_of(first + j * 64, 64), 64)
                ri = row_inv[rows, :]
                mate = mate_col[rows, :]
                w = expon[rows, cols] * (jnp.concatenate([ri, ri], axis=1) + col_inv)
                w = w - jnp.where(jnp.concatenate([mate, mate], axis=1) == ids, 2.0, 0.0)
                w = w.astype(jnp.bfloat16)
                weights[rows, cols] = w
                inner = w.astype(jnp.float32) * scores[rows, cols]
                inner = inner[:, :128] + inner[:, 128:]
                if chunk == 0:
                    sum_acc[rows, :] = inner
                else:
                    sum_acc[rows, :] += inner
                return carry

            lax.fori_loop(0, HALF // 64, weigh, 0)

        def coefs(j, carry):
            rows = pl.ds(pl.multiple_of(first + j * 64, 64), 64)
            r = rinv[rows, :]
            inner = jnp.sum(sum_acc[rows, :], axis=1, keepdims=True)
            pos_acc[rows, :] = r * r * inner
            sum_acc[rows, :] = r * temper
            return carry

        lax.fori_loop(0, HALF // 64, coefs, 0)

    def grad_piece(ahead, first):
        cols = pl.ds(pl.multiple_of(lax.rem(x + ahead, 4) * QUART, QUART), QUART)
        rows = pl.ds(first, HALF)
        d = jnp.dot(weights[rows, :], keys[:, cols], preferred_element_type=jnp.float32)
        u = sum_acc[rows, :]
        v = pos_acc[rows, :]
        return d * jnp.concatenate([u] * 3, axis=1) - emb[rows, cols] * jnp.concatenate([v] * 3, axis=1)

    rs_list = []

    def rs_message(src, dst, target):
        i = len(rs_list)
        copy = pltpu.make_async_remote_copy(
            src_ref=src, dst_ref=dst, send_sem=rs_send.at[i], recv_sem=rs_recv.at[i],
            device_id=target, device_id_type=MESH,
        )
        rs_list.append(copy)
        return copy

    far_right = rs_message(far_buf.at[0], relay_in.at[0], x_right)
    far_left = rs_message(far_buf.at[1], relay_in.at[1], x_left)
    right_bot = rs_message(near_buf.at[0], side_in.at[0], x_right)
    left_top = rs_message(near_buf.at[1], side_in.at[1], x_left)
    right_top = rs_message(near_buf.at[2], side_in.at[2], x_right)
    left_bot = rs_message(near_buf.at[3], side_in.at[3], x_left)
    cross = rs_message(cross_out, cross_in, dev_cross)
    y_first = [rs_message(yo_buf.at[a], yi_buf.at[a], dev_cross) for a in range(4)]
    x_second = {a: rs_message(xo_buf.at[a], xi_buf.at[a], {1: x_right, 2: x_far, 3: x_left}[a]) for a in (1, 2, 3)}

    lane_high = lane >= 64
    mine = lane_high == (yhi == 1)
    other = lane_high == (yhi == 0)
    f32, bf16 = jnp.float32, jnp.bfloat16

    def my_full(t0, t2):
        return jnp.where(yhi == 0, t0, t2)

    def send_y(a):
        d = grad_piece(a, HALF)
        t0, t1, t2 = d[:, :128], d[:, 128:256], d[:, 256:]
        yo_buf[a, 0:HALF, :] = my_full(t2, t0).astype(bf16)
        yo_buf[a, HALF:, :] = pack(t1, other).astype(bf16)
        y_first[a].start()
        hold_full[a] = my_full(t0, t2)
        hold_half[a] = t1

    def add_y(a):
        y_first[a].wait_recv()
        full = hold_full[a] + yi_buf[a, 0:HALF, :].astype(f32)
        half = hold_half[a] + unpack(yi_buf[a, HALF:, :].astype(f32))
        return full, half

    def send_x(a):
        full, half = add_y(a)
        xo_buf[a, 0:HALF, :] = full.astype(bf16)
        xo_buf[a, HALF:, :] = pack(half, mine).astype(bf16)
        x_second[a].start()

    weigh_rows(HALF)
    send_y(2)
    weigh_rows(0)
    d = grad_piece(2, 0)
    far_buf[0] = d[:FORTH].astype(bf16)
    far_right.start()
    far_buf[1] = d[FORTH:].astype(bf16)
    far_left.start()
    send_y(1)
    d = grad_piece(1, 0)
    near_buf[0] = d[FORTH:].astype(bf16)
    right_bot.start()
    hold_x[0] = d[:FORTH]
    d = grad_piece(3, 0)
    near_buf[1] = d[:FORTH].astype(bf16)
    left_top.start()
    hold_x[1] = d[FORTH:]
    send_y(3)
    send_y(0)
    send_x(2)
    far_right.wait_recv()
    near_buf[2] = (hold_x[0] + relay_in[0].astype(f32)).astype(bf16)
    right_top.start()
    far_left.wait_recv()
    near_buf[3] = (hold_x[1] + relay_in[1].astype(f32)).astype(bf16)
    left_bot.start()
    acc[...] = grad_piece(0, 0)
    right_bot.wait_recv()
    left_top.wait_recv()
    acc[FORTH:, :] += side_in[0].astype(f32)
    acc[:FORTH, :] += side_in[1].astype(f32)
    send_x(1)
    send_x(3)
    right_top.wait_recv()
    left_bot.wait_recv()
    acc[:FORTH, :] += side_in[2].astype(f32)
    acc[FORTH:, :] += side_in[3].astype(f32)
    t0, t1, t2 = acc[:, :128], acc[:, 128:256], acc[:, 256:]
    cross_out[0:HALF, :] = my_full(t2, t0).astype(bf16)
    cross_out[HALF:, :] = pack(t1, other).astype(bf16)
    cross.start()

    def write(first, full, half):
        rows = slice(first, first + HALF)
        full_turned = turn(full)
        grad_ref[rows, :128] = jnp.where(yhi == 0, full, jnp.where(lane_high, full_turned, turn(half)))
        grad_ref[rows, 128:] = jnp.where(yhi == 0, half, full_turned)[:, :64]

    full, half = add_y(0)
    for a in (2, 1, 3):
        x_second[a].wait_recv()
        full = full + xi_buf[a, 0:HALF, :].astype(f32)
        half = half + unpack(xi_buf[a, HALF:, :].astype(f32))
    write(HALF, full, half)
    cross.wait_recv()
    full = my_full(acc[:, :128], acc[:, 256:]) + cross_in[0:HALF, :].astype(f32)
    half = acc[:, 128:256] + unpack(cross_in[HALF:, :].astype(f32))
    write(0, full, half)
    near_all.wait_send()
    far_all.wait_send()
    stat_all.wait_send()
    for copy in rs_list:
        copy.wait_send()


def shards(embeddings, partner, inv_temp):
    f32, bf16 = jnp.float32, jnp.bfloat16
    vmem = pl.BlockSpec(memory_space=pltpu.VMEM)
    unit = HALF + FORTH
    loss, grad = pl.pallas_call(
        kernel,
        out_shape=(jax.ShapeDtypeStruct((1, ROWS), f32), jax.ShapeDtypeStruct((ROWS, 192), f32)),
        in_specs=[pl.BlockSpec(memory_space=pltpu.SMEM), vmem, pl.BlockSpec(memory_space=pl.ANY)],
        out_specs=(vmem, vmem),
        scratch_shapes=[
            pltpu.VMEM((ROWS, FEATS), f32),
            pltpu.VMEM((ROWS, FEATS), bf16),
            pltpu.VMEM((ROWS, 128), f32),
            pltpu.VMEM((KEYS, FEATS), bf16),
            pltpu.VMEM((ROWS, KEYS), f32),
            pltpu.VMEM((ROWS, KEYS), f32),
            pltpu.VMEM((ROWS, KEYS), bf16),
            pltpu.VMEM((ROWS, 128), f32),
            pltpu.VMEM((ROWS, 128), f32),
            pltpu.VMEM((ROWS, 128), f32),
            pltpu.VMEM((ROWS, 128), f32),
            pltpu.VMEM((2, ROWS), f32),
            pltpu.VMEM((8, 2, ROWS), f32),
            pltpu.VMEM((16, 128), f32),
            pltpu.VMEM((5, 16, 128), f32),
            pltpu.VMEM((16, 128), f32),
            pltpu.VMEM((8, 16, 128), f32),
            pltpu.VMEM((16, 128), f32),
            pltpu.VMEM((2, FORTH, QUART), bf16),
            pltpu.VMEM((4, FORTH, QUART), bf16),
            pltpu.VMEM((2, FORTH, QUART), bf16),
            pltpu.VMEM((4, FORTH, QUART), bf16),
            pltpu.VMEM((2, FORTH, QUART), f32),
            pltpu.VMEM((HALF, QUART), f32),
            pltpu.VMEM((4, HALF, 128), f32),
            pltpu.VMEM((4, HALF, 128), f32),
            pltpu.VMEM((4, unit, 128), bf16),
            pltpu.VMEM((4, unit, 128), bf16),
            pltpu.VMEM((unit, 128), bf16),
            pltpu.VMEM((unit, 128), bf16),
            pltpu.VMEM((4, unit, 128), bf16),
            pltpu.VMEM((4, unit, 128), bf16),
            pltpu.SemaphoreType.DMA((4,)),
            pltpu.SemaphoreType.DMA((76,)),
            pltpu.SemaphoreType.DMA((76,)),
            pltpu.SemaphoreType.DMA((2,)),
            pltpu.SemaphoreType.DMA((4,)),
            pltpu.SemaphoreType.DMA((14,)),
            pltpu.SemaphoreType.DMA((14,)),
        ],
        compiler_params=pltpu.CompilerParams(
            collective_id=0, has_side_effects=True, vmem_limit_bytes=61 * 1024 * 1024
        ),
    )(inv_temp, partner.reshape(1, ROWS), embeddings)
    return (loss.reshape(ROWS), grad)


def solution(mesh):
    in_specs = (P("blk", None), P("blk"), P())
    out_specs = (P("blk"), P("blk", "grp"))
    return jax.shard_map(shards, mesh=mesh, in_specs=in_specs, out_specs=out_specs, check_vma=False)
```

```python
import jax
import jax.numpy as jnp
from jax import lax
from jax.experimental import pallas as pl
from jax.experimental.pallas import tpu as pltpu
from jax.sharding import PartitionSpec as P

MESH = pl.DeviceIdType.MESH
ROWS = 512
FEATS = 1536
SUB = 16
CHUNK = 256
KEYS = 2048
QUART = 384
HALF = 256
FORTH = 128
ORDER = (0, 2, 1, 3)


def tile_of(dist, side, other_y):
    if dist in (0, 4):
        return (0 if dist == 0 else 14) + other_y
    return 2 * (2 * dist - 1 + other_y) + side


TILES = {}
for _d in range(5):
    for _s in (0, 1):
        for _o in (0, 1):
            if not (_d in (0, 4) and _s == 1):
                TILES[tile_of(_d, _s, _o)] = (_d, _s, _o)


def slot(dist, side, other_y, other_core, piece):
    return 128 * tile_of(dist, side, other_y) + 64 * other_core + SUB * piece


def turn(v):
    return pltpu.roll(v, 64, axis=1)


def pack(v, mask):
    n = v.shape[0] // 2
    return jnp.where(mask, v[:n], turn(v[n:]))


def unpack(m):
    return jnp.concatenate([m, turn(m)], axis=0)


def kernel(
    temp_ref, partner_ref, emb_hbm, loss_ref, grad_ref,
    emb, query, rinv, keys, scores, expon, weights, sum_acc, pos_acc, row_inv, mate_col,
    stat_out, stat_in, col_out, col_near, col_sum, col_far, key_tot,
    far_buf, near_buf, relay_in, side_in, hold_x, acc, hold_full, hold_half,
    yo_buf, yi_buf, cross_out, cross_in, xo_buf, xi_buf,
    load_sem, ag_send, ag_recv, stat_sem, col_sem, rs_send, rs_recv,
):
    blk = lax.axis_index("blk")
    grp = lax.axis_index("grp")
    ylo = lax.div(blk, 16)
    z = lax.rem(lax.div(blk, 2), 8)
    core = lax.rem(blk, 2)
    x = lax.div(grp, 2)
    yhi = lax.rem(grp, 2)
    y = yhi * 2 + ylo
    part_a = yhi
    part_b = lax.rem(yhi + ylo, 2)

    def device(x_, y_, z_, core_):
        return (lax.rem(y_, 2) * 16 + z_ * 2 + core_, x_ * 2 + lax.div(y_, 2))

    z_right = device(x, y, lax.rem(z + 1, 8), core)
    z_left = device(x, y, lax.rem(z + 7, 8), core)
    y_a = y + 1 - 2 * ylo
    y_b = 3 - y
    dev_a = device(x, y_a, z, core)
    dev_b = device(x, y_b, z, core)
    sib = device(x, y, z, 1 - core)
    x_right = device(lax.rem(x + 1, 4), y, z, core)
    x_left = device(lax.rem(x + 3, 4), y, z, core)
    x_far = device(lax.rem(x + 2, 4), y, z, core)
    dev_cross = device(x, lax.rem(y + 2, 4), z, core)
    peers = [(blk, lax.rem(grp + r, 8)) for r in range(1, 8)]

    barrier = pltpu.get_barrier_semaphore()
    greeted = [z_right, z_left, dev_a, dev_b, sib] + peers
    for target in greeted:
        pl.semaphore_signal(barrier, inc=1, device_id=target, device_id_type=MESH)

    loads = []
    for i in range(4):
        rows = pl.ds(pl.multiple_of(lax.rem(x + i, 4) * 128, 128), 128)
        copy = pltpu.make_async_copy(emb_hbm.at[rows], emb.at[rows], load_sem.at[i])
        copy.start()
        loads.append(copy)

    temper = temp_ref[0].astype(jnp.float32)

    def unit_rows(rows):
        e = emb[rows, :]
        r = lax.rsqrt(jnp.sum(e * e, axis=1, keepdims=True) + 1e-06)
        return (e * r).astype(jnp.bfloat16), r

    def normalize(i):
        first = lax.rem(x + i, 4) * 128

        def step(j, carry):
            for k in range(4):
                rows = pl.ds(pl.multiple_of(first + j * 64 + k * SUB, SUB), SUB)
                q, r = unit_rows(rows)
                query[rows, :] = q
                rinv[rows, :] = jnp.broadcast_to(r, (SUB, 128))
            return carry

        lax.fori_loop(0, 2, step, 0)

    loads[0].wait()
    for piece in range(4):
        first = x * 128 + (part_a * 32 if piece < 2 else 64 + part_b * 32) + SUB * (piece % 2)
        q, _ = unit_rows(pl.ds(pl.multiple_of(first, SUB), SUB))
        keys[SUB * piece : SUB * (piece + 1), :] = q

    pl.semaphore_wait(barrier, len(greeted))

    messages = []

    def message(src, dst, rows, target):
        i = len(messages)
        copy = pltpu.make_async_remote_copy(
            src_ref=keys.at[pl.ds(src, rows)],
            dst_ref=keys.at[pl.ds(dst, rows)],
            send_sem=ag_send.at[i],
            recv_sem=ag_recv.at[i],
            device_id=target,
            device_id_type=MESH,
        )
        messages.append(copy)
        return copy

    ring, across, twin = {}, {}, {}
    for dist in range(1, 5):
        for piece in ORDER:
            for side in (0, 1):
                if dist == 4 and side != piece // 2:
                    continue
                src = slot(dist - 1, 0 if dist == 1 else side, 0, 0, piece)
                dst = slot(dist, 0 if dist == 4 else side, 0, 0, piece)
                ring[side, dist, piece] = message(src, dst, SUB, z_right if side == 0 else z_left)
    for dist in range(5):
        for side in (0, 1):
            if dist in (0, 4) and side == 1:
                continue
            for piece in range(4):
                across[side, dist, piece] = message(
                    slot(dist, side, 0, 0, piece), slot(dist, side, 1, 0, piece), SUB, dev_a if piece < 2 else dev_b
                )
            for other in (0, 1):
                twin[side, dist, other] = message(
                    slot(dist, side, other, 0, 0), slot(dist, side, other, 1, 0), 4 * SUB, sib
                )

    lane = lax.broadcasted_iota(jnp.int32, (1, 128), 1)

    def tile_place(tile):
        dist, side, other = TILES[tile]
        return lax.rem(z + (8 - dist if side == 0 else dist), 8), other

    def key_ids(chunk):
        ids = []
        for tile in (2 * chunk, 2 * chunk + 1):
            zk, other = tile_place(tile)
            yk = ylo if other == 0 else 1 - ylo
            ck = jnp.where(lane < 64, core, 1 - core)
            within = jnp.where(lane % 64 < 32, part_a * 32, part_b * 32 + 64) + lane % 32
            ids.append((((yk * 8 + zk) * 2 + ck) * ROWS + x * 128 + within).astype(jnp.float32))
        return jnp.concatenate(ids, axis=1)

    def score_half(chunk, half):
        cols = slice(chunk * CHUNK, (chunk + 1) * CHUNK)
        rows = slice(half * HALF, (half + 1) * HALF)
        ids = key_ids(chunk)
        s = temper * lax.dot_general(
            query[rows, :], keys[cols, :], (((1,), (1,)), ((), ())), preferred_element_type=jnp.float32
        )
        e = jnp.exp(s - temper)
        if chunk == 0:
            own = lax.broadcasted_iota(jnp.int32, (HALF, CHUNK), 0) + (blk * ROWS + half * HALF)
            e = jnp.where(own.astype(jnp.float32) == ids, 0.0, e)
        mate = mate_col[rows, :]
        mate = jnp.concatenate([mate, mate], axis=1)
        p = jnp.where(mate == ids, s, 0.0)
        scores[rows, cols] = s
        expon[rows, cols] = e
        if chunk == 0:
            sum_acc[rows, :] = e[:, :128] + e[:, 128:]
            pos_acc[rows, :] = p[:, :128] + p[:, 128:]
        else:
            sum_acc[rows, :] += e[:, :128] + e[:, 128:]
            pos_acc[rows, :] += p[:, :128] + p[:, 128:]
        total = jnp.sum(e, axis=0, keepdims=True)
        for i in (0, 1):
            zk, other = tile_place(2 * chunk + i)
            row = pl.ds(other * 8 + zk, 1)
            part = total[:, 128 * i : 128 * (i + 1)]
            if half == 0:
                col_out[row, :] = part
            else:
                col_out[row, :] += part

    for piece in ORDER:
        for side in (0, 1):
            ring[side, 1, piece].start()
        across[0, 0, piece].start()
    twin[0, 0, 0].start()
    normalize(0)
    loads[1].wait()
    normalize(1)

    def sides(dist):
        return (0,) if dist in (0, 4) else (0, 1)

    def finish_across(dist):
        for side in sides(dist):
            for piece in ORDER:
                across[side, dist, piece].wait_recv()
            twin[side, dist, 1].start()

    def finish_twin(dist, other):
        for side in sides(dist):
            twin[side, dist, other].wait_recv()

    def meanwhile(dist, turn_):
        if dist == 1:
            if turn_ == 0:
                loads[2].wait()
                normalize(2)
            elif turn_ == 1:
                loads[3].wait()
                normalize(3)
                mate_row = jnp.broadcast_to(partner_ref[...].astype(jnp.float32), (128, ROWS))
                mate_col[...] = mate_row.T
            elif turn_ == 2:
                finish_across(0)
            else:
                finish_twin(0, 0)
                finish_twin(0, 1)
                score_half(0, 0)
        elif turn_ == 0:
            score_half(2 * (dist - 2), 1)
        elif turn_ == 1:
            finish_twin(dist - 1, 0)
            score_half(2 * (dist - 1) - 1, 0)
        elif turn_ == 2:
            score_half(2 * (dist - 1) - 1, 1)
            finish_across(dist - 1)
        else:
            finish_twin(dist - 1, 1)
            score_half(2 * (dist - 1), 0)

    for dist in range(1, 4):
        for turn_, piece in enumerate(ORDER):
            for side in (0, 1):
                ring[side, dist, piece].wait_recv()
                if dist < 3 or side == piece // 2:
                    ring[side, dist + 1, piece].start()
                across[side, dist, piece].start()
                if turn_ == 3:
                    twin[side, dist, 0].start()
            meanwhile(dist, turn_)
    for piece in (0, 2):
        ring[piece // 2, 4, piece].wait_recv()
        across[0, 4, piece].start()
    meanwhile(4, 0)
    for piece in (1, 3):
        ring[piece // 2, 4, piece].wait_recv()
        across[0, 4, piece].start()
    twin[0, 4, 0].start()
    meanwhile(4, 1)
    meanwhile(4, 2)
    meanwhile(4, 3)
    score_half(6, 1)
    finish_across(4)
    finish_twin(4, 0)
    finish_twin(4, 1)
    score_half(7, 0)
    score_half(7, 1)

    def small(src, dst, sems, i, target):
        return pltpu.make_async_remote_copy(
            src_ref=src, dst_ref=dst, send_sem=sems.at[i], recv_sem=sems.at[i + 1],
            device_id=target, device_id_type=MESH,
        )

    near_targets = [sib, dev_a, dev_b, device(x, y_a, z, 1 - core), device(x, y_b, z, 1 - core)]
    for i, target in enumerate(near_targets):
        small(col_out, col_near.at[i], col_sem, 0, target).start()
    stat_out[0:1, :] = jnp.sum(sum_acc[...].T, axis=0, keepdims=True)
    stat_out[1:2, :] = jnp.sum(pos_acc[...].T, axis=0, keepdims=True)
    for r in range(1, 8):
        small(stat_out, stat_in.at[r], stat_sem, 0, peers[r - 1]).start()
    near_all = small(col_near, col_near, col_sem, 0, sib)
    near_all.wait_recv()
    is_a = lax.broadcasted_iota(jnp.int32, (16, 128), 1) % 64 < 32

    def flip(v):
        return jnp.concatenate([v[8:], v[:8]], axis=0)

    over_a = flip(col_near[1] + turn(col_near[3]))
    over_b = flip(col_near[2] + turn(col_near[4]))
    col_sum[...] = col_out[...] + turn(col_near[0]) + jnp.where(is_a, over_a, over_b)
    for dz in range(1, 8):
        small(col_sum, col_far.at[dz], col_sem, 2, device(x, y, lax.rem(z + dz, 8), core)).start()
    for copy in messages:
        copy.wait_send()
    stat_all = small(stat_in.at[pl.ds(1, 7)], stat_in.at[pl.ds(1, 7)], stat_sem, 0, peers[0])
    stat_all.wait_recv()
    total = stat_out[...]
    for r in range(1, 8):
        total = total + stat_in[r]
    sums = total[0:1, :]
    inverse = 1.0 / sums
    loss_ref[...] = temper + jnp.log(sums) - total[1:2, :]
    for i in range(4):
        part = slice(128 * i, 128 * (i + 1))
        row_inv[part, :] = jnp.broadcast_to(inverse[:, part], (128, 128)).T
    far_all = small(col_far.at[pl.ds(1, 7)], col_far.at[pl.ds(1, 7)], col_sem, 2, z_right)
    far_all.wait_recv()
    col_total = col_sum[...]
    for dz in range(1, 8):
        col_total = col_total + col_far[dz]
    key_tot[...] = 1.0 / col_total

    def weigh_rows(first):
        for chunk in range(8):
            cols = slice(chunk * CHUNK, (chunk + 1) * CHUNK)
            ids = key_ids(chunk)
            inv = []
            for tile in (2 * chunk, 2 * chunk + 1):
                zk, other = tile_place(tile)
                inv.append(key_tot[pl.ds(other * 8 + zk, 1), :])
            col_inv = jnp.concatenate(inv, axis=1)

            def weigh(j, carry, cols=cols, ids=ids, col_inv=col_inv, chunk=chunk):
                rows = pl.ds(pl.multiple_of(first + j * 64, 64), 64)
                ri = row_inv[rows, :]
                mate = mate_col[rows, :]
                w = expon[rows, cols] * (jnp.concatenate([ri, ri], axis=1) + col_inv)
                w = w - jnp.where(jnp.concatenate([mate, mate], axis=1) == ids, 2.0, 0.0)
                w = w.astype(jnp.bfloat16)
                weights[rows, cols] = w
                inner = w.astype(jnp.float32) * scores[rows, cols]
                inner = inner[:, :128] + inner[:, 128:]
                if chunk == 0:
                    sum_acc[rows, :] = inner
                else:
                    sum_acc[rows, :] += inner
                return carry

            lax.fori_loop(0, HALF // 64, weigh, 0)

        def coefs(j, carry):
            rows = pl.ds(pl.multiple_of(first + j * 64, 64), 64)
            r = rinv[rows, :]
            inner = jnp.sum(sum_acc[rows, :], axis=1, keepdims=True)
            pos_acc[rows, :] = r * r * inner
            sum_acc[rows, :] = r * temper
            return carry

        lax.fori_loop(0, HALF // 64, coefs, 0)

    def grad_piece(ahead, first):
        cols = pl.ds(pl.multiple_of(lax.rem(x + ahead, 4) * QUART, QUART), QUART)
        rows = pl.ds(first, HALF)
        d = jnp.dot(weights[rows, :], keys[:, cols], preferred_element_type=jnp.float32)
        u = sum_acc[rows, :]
        v = pos_acc[rows, :]
        return d * jnp.concatenate([u] * 3, axis=1) - emb[rows, cols] * jnp.concatenate([v] * 3, axis=1)

    rs_list = []

    def rs_message(src, dst, target):
        i = len(rs_list)
        copy = pltpu.make_async_remote_copy(
            src_ref=src, dst_ref=dst, send_sem=rs_send.at[i], recv_sem=rs_recv.at[i],
            device_id=target, device_id_type=MESH,
        )
        rs_list.append(copy)
        return copy

    far_right = rs_message(far_buf.at[0], relay_in.at[0], x_right)
    far_left = rs_message(far_buf.at[1], relay_in.at[1], x_left)
    right_bot = rs_message(near_buf.at[0], side_in.at[0], x_right)
    left_top = rs_message(near_buf.at[1], side_in.at[1], x_left)
    right_top = rs_message(near_buf.at[2], side_in.at[2], x_right)
    left_bot = rs_message(near_buf.at[3], side_in.at[3], x_left)
    cross = rs_message(cross_out, cross_in, dev_cross)
    y_first = [rs_message(yo_buf.at[a], yi_buf.at[a], dev_cross) for a in range(4)]
    x_second = {a: rs_message(xo_buf.at[a], xi_buf.at[a], {1: x_right, 2: x_far, 3: x_left}[a]) for a in (1, 2, 3)}

    lane_high = lane >= 64
    mine = lane_high == (yhi == 1)
    other = lane_high == (yhi == 0)
    f32, bf16 = jnp.float32, jnp.bfloat16

    def my_full(t0, t2):
        return jnp.where(yhi == 0, t0, t2)

    def send_y(a):
        d = grad_piece(a, HALF)
        t0, t1, t2 = d[:, :128], d[:, 128:256], d[:, 256:]
        yo_buf[a, 0:HALF, :] = my_full(t2, t0).astype(bf16)
        yo_buf[a, HALF:, :] = pack(t1, other).astype(bf16)
        y_first[a].start()
        hold_full[a] = my_full(t0, t2)
        hold_half[a] = t1

    def add_y(a):
        y_first[a].wait_recv()
        full = hold_full[a] + yi_buf[a, 0:HALF, :].astype(f32)
        half = hold_half[a] + unpack(yi_buf[a, HALF:, :].astype(f32))
        return full, half

    def send_x(a):
        full, half = add_y(a)
        xo_buf[a, 0:HALF, :] = full.astype(bf16)
        xo_buf[a, HALF:, :] = pack(half, mine).astype(bf16)
        x_second[a].start()

    weigh_rows(HALF)
    send_y(2)
    weigh_rows(0)
    d = grad_piece(2, 0)
    far_buf[0] = d[:FORTH].astype(bf16)
    far_right.start()
    far_buf[1] = d[FORTH:].astype(bf16)
    far_left.start()
    send_y(1)
    d = grad_piece(1, 0)
    near_buf[0] = d[FORTH:].astype(bf16)
    right_bot.start()
    hold_x[0] = d[:FORTH]
    d = grad_piece(3, 0)
    near_buf[1] = d[:FORTH].astype(bf16)
    left_top.start()
    hold_x[1] = d[FORTH:]
    send_y(3)
    send_y(0)
    send_x(2)
    far_right.wait_recv()
    near_buf[2] = (hold_x[0] + relay_in[0].astype(f32)).astype(bf16)
    right_top.start()
    far_left.wait_recv()
    near_buf[3] = (hold_x[1] + relay_in[1].astype(f32)).astype(bf16)
    left_bot.start()
    acc[...] = grad_piece(0, 0)
    right_bot.wait_recv()
    left_top.wait_recv()
    acc[FORTH:, :] += side_in[0].astype(f32)
    acc[:FORTH, :] += side_in[1].astype(f32)
    send_x(1)
    send_x(3)
    right_top.wait_recv()
    left_bot.wait_recv()
    acc[:FORTH, :] += side_in[2].astype(f32)
    acc[FORTH:, :] += side_in[3].astype(f32)
    t0, t1, t2 = acc[:, :128], acc[:, 128:256], acc[:, 256:]
    cross_out[0:HALF, :] = my_full(t2, t0).astype(bf16)
    cross_out[HALF:, :] = pack(t1, other).astype(bf16)
    cross.start()

    def write(first, full, half):
        rows = slice(first, first + HALF)
        full_turned = turn(full)
        grad_ref[rows, :128] = jnp.where(yhi == 0, full, jnp.where(lane_high, full_turned, turn(half)))
        grad_ref[rows, 128:] = jnp.where(yhi == 0, half, full_turned)[:, :64]

    full, half = add_y(0)
    for a in (2, 1, 3):
        x_second[a].wait_recv()
        full = full + xi_buf[a, 0:HALF, :].astype(f32)
        half = half + unpack(xi_buf[a, HALF:, :].astype(f32))
    write(HALF, full, half)
    cross.wait_recv()
    full = my_full(acc[:, :128], acc[:, 256:]) + cross_in[0:HALF, :].astype(f32)
    half = acc[:, 128:256] + unpack(cross_in[HALF:, :].astype(f32))
    write(0, full, half)
    near_all.wait_send()
    far_all.wait_send()
    stat_all.wait_send()
    for copy in rs_list:
        copy.wait_send()


def shards(embeddings, partner, inv_temp):
    f32, bf16 = jnp.float32, jnp.bfloat16
    vmem = pl.BlockSpec(memory_space=pltpu.VMEM)
    unit = HALF + FORTH
    loss, grad = pl.pallas_call(
        kernel,
        out_shape=(jax.ShapeDtypeStruct((1, ROWS), f32), jax.ShapeDtypeStruct((ROWS, 192), f32)),
        in_specs=[pl.BlockSpec(memory_space=pltpu.SMEM), vmem, pl.BlockSpec(memory_space=pltpu.HBM)],
        out_specs=(vmem, vmem),
        scratch_shapes=[
            pltpu.VMEM((ROWS, FEATS), f32),
            pltpu.VMEM((ROWS, FEATS), bf16),
            pltpu.VMEM((ROWS, 128), f32),
            pltpu.VMEM((KEYS, FEATS), bf16),
            pltpu.VMEM((ROWS, KEYS), f32),
            pltpu.VMEM((ROWS, KEYS), f32),
            pltpu.VMEM((ROWS, KEYS), bf16),
            pltpu.VMEM((ROWS, 128), f32),
            pltpu.VMEM((ROWS, 128), f32),
            pltpu.VMEM((ROWS, 128), f32),
            pltpu.VMEM((ROWS, 128), f32),
            pltpu.VMEM((2, ROWS), f32),
            pltpu.VMEM((8, 2, ROWS), f32),
            pltpu.VMEM((16, 128), f32),
            pltpu.VMEM((5, 16, 128), f32),
            pltpu.VMEM((16, 128), f32),
            pltpu.VMEM((8, 16, 128), f32),
            pltpu.VMEM((16, 128), f32),
            pltpu.VMEM((2, FORTH, QUART), bf16),
            pltpu.VMEM((4, FORTH, QUART), bf16),
            pltpu.VMEM((2, FORTH, QUART), bf16),
            pltpu.VMEM((4, FORTH, QUART), bf16),
            pltpu.VMEM((2, FORTH, QUART), f32),
            pltpu.VMEM((HALF, QUART), f32),
            pltpu.VMEM((4, HALF, 128), f32),
            pltpu.VMEM((4, HALF, 128), f32),
            pltpu.VMEM((4, unit, 128), bf16),
            pltpu.VMEM((4, unit, 128), bf16),
            pltpu.VMEM((unit, 128), bf16),
            pltpu.VMEM((unit, 128), bf16),
            pltpu.VMEM((4, unit, 128), bf16),
            pltpu.VMEM((4, unit, 128), bf16),
            pltpu.SemaphoreType.DMA((4,)),
            pltpu.SemaphoreType.DMA((76,)),
            pltpu.SemaphoreType.DMA((76,)),
            pltpu.SemaphoreType.DMA((2,)),
            pltpu.SemaphoreType.DMA((4,)),
            pltpu.SemaphoreType.DMA((14,)),
            pltpu.SemaphoreType.DMA((14,)),
        ],
        compiler_params=pltpu.CompilerParams(
            collective_id=0, has_side_effects=True, vmem_limit_bytes=53 * 1024 * 1024
        ),
    )(inv_temp, partner.reshape(1, ROWS), embeddings)
    return (loss.reshape(ROWS), grad)


def solution(mesh):
    in_specs = (P("blk", None), P("blk"), P())
    out_specs = (P("blk"), P("blk", "grp"))
    return jax.shard_map(shards, mesh=mesh, in_specs=in_specs, out_specs=out_specs, check_vma=False)
```

```python
import jax
import jax.numpy as jnp
from jax import lax
from jax.experimental import pallas as pl
from jax.experimental.pallas import tpu as pltpu
from jax.sharding import PartitionSpec as P

MESH = pl.DeviceIdType.MESH
ROWS = 512
FEATS = 1536
SUB = 16
CHUNK = 256
KEYS = 2048
QUART = 384
HALF = 256
FORTH = 128
ORDER = (0, 2, 1, 3)


def tile_of(dist, side, other_y):
    if dist in (0, 4):
        return (0 if dist == 0 else 14) + other_y
    return 2 * (2 * dist - 1 + other_y) + side


TILES = {}
for _d in range(5):
    for _s in (0, 1):
        for _o in (0, 1):
            if not (_d in (0, 4) and _s == 1):
                TILES[tile_of(_d, _s, _o)] = (_d, _s, _o)


def slot(dist, side, other_y, other_core, piece):
    return 128 * tile_of(dist, side, other_y) + 64 * other_core + SUB * piece


def turn(v):
    return pltpu.roll(v, 64, axis=1)


def pack(v, mask):
    n = v.shape[0] // 2
    return jnp.where(mask, v[:n], turn(v[n:]))


def unpack(m):
    return jnp.concatenate([m, turn(m)], axis=0)


def kernel(
    temp_ref, partner_ref, emb_hbm, loss_ref, grad_ref,
    emb, query, rinv, keys, scores, expon, weights, sum_acc, pos_acc, row_inv, mate_col,
    stat_out, stat_in, col_out, col_near, col_sum, col_far, key_tot,
    far_buf, near_buf, relay_in, side_in, hold_x, acc, hold_full, hold_half,
    yo_buf, yi_buf, cross_out, cross_in, xo_buf, xi_buf,
    load_sem, ag_send, ag_recv, stat_sem, col_sem, rs_send, rs_recv,
):
    blk = lax.axis_index("blk")
    grp = lax.axis_index("grp")
    ylo = lax.div(blk, 16)
    z = lax.rem(lax.div(blk, 2), 8)
    core = lax.rem(blk, 2)
    x = lax.div(grp, 2)
    yhi = lax.rem(grp, 2)
    y = yhi * 2 + ylo
    part_a = yhi
    part_b = lax.rem(yhi + ylo, 2)

    def device(x_, y_, z_, core_):
        return (lax.rem(y_, 2) * 16 + z_ * 2 + core_, x_ * 2 + lax.div(y_, 2))

    z_right = device(x, y, lax.rem(z + 1, 8), core)
    z_left = device(x, y, lax.rem(z + 7, 8), core)
    y_a = y + 1 - 2 * ylo
    y_b = 3 - y
    dev_a = device(x, y_a, z, core)
    dev_b = device(x, y_b, z, core)
    sib = device(x, y, z, 1 - core)
    x_right = device(lax.rem(x + 1, 4), y, z, core)
    x_left = device(lax.rem(x + 3, 4), y, z, core)
    x_far = device(lax.rem(x + 2, 4), y, z, core)
    dev_cross = device(x, lax.rem(y + 2, 4), z, core)
    peers = [(blk, lax.rem(grp + r, 8)) for r in range(1, 8)]

    barrier = pltpu.get_barrier_semaphore()
    greeted = [z_right, z_left, dev_a, dev_b, sib] + peers
    for target in greeted:
        pl.semaphore_signal(barrier, inc=1, device_id=target, device_id_type=MESH)

    loads = []
    for i in range(4):
        rows = pl.ds(pl.multiple_of(lax.rem(x + i, 4) * 128, 128), 128)
        copy = pltpu.make_async_copy(emb_hbm.at[rows], emb.at[rows], load_sem.at[i])
        copy.start()
        loads.append(copy)

    temper = temp_ref[0].astype(jnp.float32)

    def unit_rows(rows):
        e = emb[rows, :]
        r = lax.rsqrt(jnp.sum(e * e, axis=1, keepdims=True) + 1e-06)
        return (e * r).astype(jnp.bfloat16), r

    def normalize(i):
        first = lax.rem(x + i, 4) * 128

        def step(j, carry):
            for k in range(4):
                rows = pl.ds(pl.multiple_of(first + j * 64 + k * SUB, SUB), SUB)
                q, r = unit_rows(rows)
                query[rows, :] = q
                rinv[rows, :] = jnp.broadcast_to(r, (SUB, 128))
            return carry

        lax.fori_loop(0, 2, step, 0)

    loads[0].wait()
    for piece in range(4):
        first = x * 128 + (part_a * 32 if piece < 2 else 64 + part_b * 32) + SUB * (piece % 2)
        q, _ = unit_rows(pl.ds(pl.multiple_of(first, SUB), SUB))
        keys[SUB * piece : SUB * (piece + 1), :] = q

    pl.semaphore_wait(barrier, len(greeted))

    messages = []

    def message(src, dst, rows, target):
        i = len(messages)
        copy = pltpu.make_async_remote_copy(
            src_ref=keys.at[pl.ds(src, rows)],
            dst_ref=keys.at[pl.ds(dst, rows)],
            send_sem=ag_send.at[i],
            recv_sem=ag_recv.at[i],
            device_id=target,
            device_id_type=MESH,
        )
        messages.append(copy)
        return copy

    ring, across, twin = {}, {}, {}
    for dist in range(1, 5):
        for piece in ORDER:
            for side in (0, 1):
                if dist == 4 and side != piece // 2:
                    continue
                src = slot(dist - 1, 0 if dist == 1 else side, 0, 0, piece)
                dst = slot(dist, 0 if dist == 4 else side, 0, 0, piece)
                ring[side, dist, piece] = message(src, dst, SUB, z_right if side == 0 else z_left)
    for dist in range(5):
        for side in (0, 1):
            if dist in (0, 4) and side == 1:
                continue
            for piece in range(4):
                across[side, dist, piece] = message(
                    slot(dist, side, 0, 0, piece), slot(dist, side, 1, 0, piece), SUB, dev_a if piece < 2 else dev_b
                )
            for other in (0, 1):
                twin[side, dist, other] = message(
                    slot(dist, side, other, 0, 0), slot(dist, side, other, 1, 0), 4 * SUB, sib
                )

    lane = lax.broadcasted_iota(jnp.int32, (1, 128), 1)

    def tile_place(tile):
        dist, side, other = TILES[tile]
        return lax.rem(z + (8 - dist if side == 0 else dist), 8), other

    def key_ids(chunk):
        ids = []
        for tile in (2 * chunk, 2 * chunk + 1):
            zk, other = tile_place(tile)
            yk = ylo if other == 0 else 1 - ylo
            ck = jnp.where(lane < 64, core, 1 - core)
            within = jnp.where(lane % 64 < 32, part_a * 32, part_b * 32 + 64) + lane % 32
            ids.append((((yk * 8 + zk) * 2 + ck) * ROWS + x * 128 + within).astype(jnp.float32))
        return jnp.concatenate(ids, axis=1)

    def score_half(chunk, half):
        cols = slice(chunk * CHUNK, (chunk + 1) * CHUNK)
        rows = slice(half * HALF, (half + 1) * HALF)
        ids = key_ids(chunk)
        s = temper * lax.dot_general(
            query[rows, :], keys[cols, :], (((1,), (1,)), ((), ())), preferred_element_type=jnp.float32
        )
        e = jnp.exp(s - temper)
        if chunk == 0:
            own = lax.broadcasted_iota(jnp.int32, (HALF, CHUNK), 0) + (blk * ROWS + half * HALF)
            e = jnp.where(own.astype(jnp.float32) == ids, 0.0, e)
        mate = mate_col[rows, :]
        mate = jnp.concatenate([mate, mate], axis=1)
        p = jnp.where(mate == ids, s, 0.0)
        scores[rows, cols] = s
        expon[rows, cols] = e
        if chunk == 0:
            sum_acc[rows, :] = e[:, :128] + e[:, 128:]
            pos_acc[rows, :] = p[:, :128] + p[:, 128:]
        else:
            sum_acc[rows, :] += e[:, :128] + e[:, 128:]
            pos_acc[rows, :] += p[:, :128] + p[:, 128:]
        total = jnp.sum(e, axis=0, keepdims=True)
        for i in (0, 1):
            zk, other = tile_place(2 * chunk + i)
            row = pl.ds(other * 8 + zk, 1)
            part = total[:, 128 * i : 128 * (i + 1)]
            if half == 0:
                col_out[row, :] = part
            else:
                col_out[row, :] += part

    for piece in ORDER:
        for side in (0, 1):
            ring[side, 1, piece].start()
        across[0, 0, piece].start()
    twin[0, 0, 0].start()
    normalize(0)
    loads[1].wait()
    normalize(1)

    def sides(dist):
        return (0,) if dist in (0, 4) else (0, 1)

    def finish_across(dist):
        for side in sides(dist):
            for piece in ORDER:
                across[side, dist, piece].wait_recv()
            twin[side, dist, 1].start()

    def finish_twin(dist, other):
        for side in sides(dist):
            twin[side, dist, other].wait_recv()

    def meanwhile(dist, turn_):
        if dist == 1:
            if turn_ == 0:
                loads[2].wait()
                normalize(2)
            elif turn_ == 1:
                loads[3].wait()
                normalize(3)
                mate_row = jnp.broadcast_to(partner_ref[...].astype(jnp.float32), (128, ROWS))
                mate_col[...] = mate_row.T
            elif turn_ == 2:
                finish_across(0)
            else:
                finish_twin(0, 0)
                finish_twin(0, 1)
                score_half(0, 0)
        elif turn_ == 0:
            score_half(2 * (dist - 2), 1)
        elif turn_ == 1:
            finish_twin(dist - 1, 0)
            score_half(2 * (dist - 1) - 1, 0)
        elif turn_ == 2:
            score_half(2 * (dist - 1) - 1, 1)
            finish_across(dist - 1)
        else:
            finish_twin(dist - 1, 1)
            score_half(2 * (dist - 1), 0)

    for dist in range(1, 4):
        for turn_, piece in enumerate(ORDER):
            for side in (0, 1):
                ring[side, dist, piece].wait_recv()
                if dist < 3 or side == piece // 2:
                    ring[side, dist + 1, piece].start()
                across[side, dist, piece].start()
                if turn_ == 3:
                    twin[side, dist, 0].start()
            meanwhile(dist, turn_)
    for piece in (0, 2):
        ring[piece // 2, 4, piece].wait_recv()
        across[0, 4, piece].start()
    meanwhile(4, 0)
    for piece in (1, 3):
        ring[piece // 2, 4, piece].wait_recv()
        across[0, 4, piece].start()
    twin[0, 4, 0].start()
    meanwhile(4, 1)
    meanwhile(4, 2)
    meanwhile(4, 3)
    score_half(6, 1)
    finish_across(4)
    finish_twin(4, 0)
    finish_twin(4, 1)
    score_half(7, 0)
    score_half(7, 1)

    def small(src, dst, sems, i, target):
        return pltpu.make_async_remote_copy(
            src_ref=src, dst_ref=dst, send_sem=sems.at[i], recv_sem=sems.at[i + 1],
            device_id=target, device_id_type=MESH,
        )

    near_targets = [sib, dev_a, dev_b, device(x, y_a, z, 1 - core), device(x, y_b, z, 1 - core)]
    for i, target in reversed(list(enumerate(near_targets))):
        small(col_out, col_near.at[i], col_sem, 0, target).start()
    stat_out[0:1, :] = jnp.sum(sum_acc[...].T, axis=0, keepdims=True)
    stat_out[1:2, :] = jnp.sum(pos_acc[...].T, axis=0, keepdims=True)
    for r in range(1, 8):
        small(stat_out, stat_in.at[r], stat_sem, 0, peers[r - 1]).start()
    near_all = small(col_near, col_near, col_sem, 0, sib)
    near_all.wait_recv()
    is_a = lax.broadcasted_iota(jnp.int32, (16, 128), 1) % 64 < 32

    def flip(v):
        return jnp.concatenate([v[8:], v[:8]], axis=0)

    over_a = flip(col_near[1] + turn(col_near[3]))
    over_b = flip(col_near[2] + turn(col_near[4]))
    col_sum[...] = col_out[...] + turn(col_near[0]) + jnp.where(is_a, over_a, over_b)
    for dz in range(1, 8):
        small(col_sum, col_far.at[dz], col_sem, 2, device(x, y, lax.rem(z + dz, 8), core)).start()
    stat_all = small(stat_in.at[pl.ds(1, 7)], stat_in.at[pl.ds(1, 7)], stat_sem, 0, peers[0])
    stat_all.wait_recv()
    total = stat_out[...]
    for r in range(1, 8):
        total = total + stat_in[r]
    sums = total[0:1, :]
    inverse = 1.0 / sums
    loss_ref[...] = temper + jnp.log(sums) - total[1:2, :]
    for i in range(4):
        part = slice(128 * i, 128 * (i + 1))
        row_inv[part, :] = jnp.broadcast_to(inverse[:, part], (128, 128)).T
    far_all = small(col_far.at[pl.ds(1, 7)], col_far.at[pl.ds(1, 7)], col_sem, 2, z_right)
    far_all.wait_recv()
    col_total = col_sum[...]
    for dz in range(1, 8):
        col_total = col_total + col_far[dz]
    key_tot[...] = 1.0 / col_total

    def weigh_rows(first):
        for chunk in range(8):
            cols = slice(chunk * CHUNK, (chunk + 1) * CHUNK)
            ids = key_ids(chunk)
            inv = []
            for tile in (2 * chunk, 2 * chunk + 1):
                zk, other = tile_place(tile)
                inv.append(key_tot[pl.ds(other * 8 + zk, 1), :])
            col_inv = jnp.concatenate(inv, axis=1)

            def weigh(j, carry, cols=cols, ids=ids, col_inv=col_inv, chunk=chunk):
                rows = pl.ds(pl.multiple_of(first + j * 64, 64), 64)
                ri = row_inv[rows, :]
                mate = mate_col[rows, :]
                w = expon[rows, cols] * (jnp.concatenate([ri, ri], axis=1) + col_inv)
                w = w - jnp.where(jnp.concatenate([mate, mate], axis=1) == ids, 2.0, 0.0)
                w = w.astype(jnp.bfloat16)
                weights[rows, cols] = w
                inner = w.astype(jnp.float32) * scores[rows, cols]
                inner = inner[:, :128] + inner[:, 128:]
                if chunk == 0:
                    sum_acc[rows, :] = inner
                else:
                    sum_acc[rows, :] += inner
                return carry

            lax.fori_loop(0, FORTH // 64, weigh, 0)

        def coefs(j, carry):
            rows = pl.ds(pl.multiple_of(first + j * 64, 64), 64)
            r = rinv[rows, :]
            inner = jnp.sum(sum_acc[rows, :], axis=1, keepdims=True)
            pos_acc[rows, :] = r * r * inner
            sum_acc[rows, :] = r * temper
            return carry

        lax.fori_loop(0, FORTH // 64, coefs, 0)

    def grad_piece(ahead, first):
        cols = pl.ds(pl.multiple_of(lax.rem(x + ahead, 4) * QUART, QUART), QUART)
        rows = pl.ds(first, FORTH)
        d = jnp.dot(weights[rows, :], keys[:, cols], preferred_element_type=jnp.float32)
        u = sum_acc[rows, :]
        v = pos_acc[rows, :]
        return d * jnp.concatenate([u] * 3, axis=1) - emb[rows, cols] * jnp.concatenate([v] * 3, axis=1)

    rs_list = []

    def rs_message(src, dst, target):
        i = len(rs_list)
        copy = pltpu.make_async_remote_copy(
            src_ref=src, dst_ref=dst, send_sem=rs_send.at[i], recv_sem=rs_recv.at[i],
            device_id=target, device_id_type=MESH,
        )
        rs_list.append(copy)
        return copy

    lane_high = lane >= 64
    mine = lane_high == (yhi == 1)
    other = lane_high == (yhi == 0)
    f32, bf16 = jnp.float32, jnp.bfloat16

    def my_full(t0, t2):
        return jnp.where(yhi == 0, t0, t2)

    def write(first, full, half):
        rows = slice(first, first + FORTH)
        full, half = full.T, half.T
        grad_ref[0:64, rows] = jnp.where(yhi == 0, full[:64], half[64:])
        grad_ref[64:128, rows] = jnp.where(yhi == 0, full[64:], full[:64])
        grad_ref[128:192, rows] = jnp.where(yhi == 0, half[:64], full[64:])

    top, bot = slice(0, FORTH // 2), slice(FORTH // 2, FORTH)
    far_right, far_left, right_bot, left_top, right_top, left_bot, cross = ([] for _ in range(7))
    for q in (0, 1):
        far_right.append(rs_message(far_buf.at[q, 0], relay_in.at[q, 0], x_right))
        far_left.append(rs_message(far_buf.at[q, 1], relay_in.at[q, 1], x_left))
        right_bot.append(rs_message(near_buf.at[q, 0], side_in.at[q, 0], x_right))
        left_top.append(rs_message(near_buf.at[q, 1], side_in.at[q, 1], x_left))
        right_top.append(rs_message(near_buf.at[q, 2], side_in.at[q, 2], x_right))
        left_bot.append(rs_message(near_buf.at[q, 3], side_in.at[q, 3], x_left))
        cross.append(rs_message(cross_out.at[q], cross_in.at[q], dev_cross))

    def x_far_parts(q):
        d = grad_piece(2, FORTH * q)
        far_buf[q, 0] = d[top].astype(bf16)
        far_right[q].start()
        far_buf[q, 1] = d[bot].astype(bf16)
        far_left[q].start()

    def x_near_parts(q):
        d = grad_piece(1, FORTH * q)
        near_buf[q, 0] = d[bot].astype(bf16)
        right_bot[q].start()
        hold_x[q, 0] = d[top]
        d = grad_piece(3, FORTH * q)
        near_buf[q, 1] = d[top].astype(bf16)
        left_top[q].start()
        hold_x[q, 1] = d[bot]

    def x_relay(q):
        far_right[q].wait_recv()
        near_buf[q, 2] = (hold_x[q, 0] + relay_in[q, 0].astype(f32)).astype(bf16)
        right_top[q].start()
        far_left[q].wait_recv()
        near_buf[q, 3] = (hold_x[q, 1] + relay_in[q, 1].astype(f32)).astype(bf16)
        left_bot[q].start()

    def x_own(q):
        acc[q] = grad_piece(0, FORTH * q)

    def x_sum(q):
        for copies in (right_bot, left_top, right_top, left_bot):
            copies[q].wait_recv()
        high = acc[q, top, :] + side_in[q, 1].astype(f32) + side_in[q, 2].astype(f32)
        low = acc[q, bot, :] + side_in[q, 0].astype(f32) + side_in[q, 3].astype(f32)
        d = jnp.concatenate([high, low], axis=0)
        t0, t1, t2 = d[:, :128], d[:, 128:256], d[:, 256:]
        cross_out[q, 0:FORTH, :] = my_full(t2, t0).astype(bf16)
        cross_out[q, FORTH:, :] = pack(t1, other).astype(bf16)
        cross[q].start()
        acc[q, :, 0:128] = my_full(t0, t2)
        acc[q, :, 128:256] = t1

    def x_finish(q):
        cross[q].wait_recv()
        full = acc[q, :, 0:128] + cross_in[q, 0:FORTH, :].astype(f32)
        half = acc[q, :, 128:256] + unpack(cross_in[q, FORTH:, :].astype(f32))
        write(FORTH * q, full, half)

    y_first = [[rs_message(yo_buf.at[q, a], yi_buf.at[q, a], dev_cross) for a in range(4)] for q in (0, 1)]
    to = {1: x_right, 2: x_far, 3: x_left}
    x_second = [{a: rs_message(xo_buf.at[q, a], xi_buf.at[q, a], to[a]) for a in (1, 2, 3)} for q in (0, 1)]

    def y_send(q, a):
        d = grad_piece(a, HALF + FORTH * q)
        t0, t1, t2 = d[:, :128], d[:, 128:256], d[:, 256:]
        yo_buf[q, a, 0:FORTH, :] = my_full(t2, t0).astype(bf16)
        yo_buf[q, a, FORTH:, :] = pack(t1, other).astype(bf16)
        y_first[q][a].start()
        hold_full[q, a] = my_full(t0, t2)
        hold_half[q, a] = t1

    def y_add(q, a):
        y_first[q][a].wait_recv()
        full = hold_full[q, a] + yi_buf[q, a, 0:FORTH, :].astype(f32)
        half = hold_half[q, a] + unpack(yi_buf[q, a, FORTH:, :].astype(f32))
        return full, half

    def y_then_x(q, a):
        full, half = y_add(q, a)
        xo_buf[q, a, 0:FORTH, :] = full.astype(bf16)
        xo_buf[q, a, FORTH:, :] = pack(half, mine).astype(bf16)
        x_second[q][a].start()

    def y_finish(q):
        full, half = y_add(q, 0)
        for a in (2, 1, 3):
            x_second[q][a].wait_recv()
            full = full + xi_buf[q, a, 0:FORTH, :].astype(f32)
            half = half + unpack(xi_buf[q, a, FORTH:, :].astype(f32))
        write(HALF + FORTH * q, full, half)

    weigh_rows(0)
    x_far_parts(0)
    weigh_rows(HALF)
    y_send(0, 2)
    y_send(0, 1)
    weigh_rows(FORTH)
    x_far_parts(1)
    x_near_parts(0)
    y_send(0, 3)
    x_relay(0)
    weigh_rows(HALF + FORTH)
    y_send(1, 2)
    x_near_parts(1)
    x_relay(1)
    y_send(1, 1)
    y_send(1, 3)
    y_send(0, 0)
    y_send(1, 0)
    x_own(0)
    x_sum(0)
    y_then_x(0, 2)
    x_own(1)
    x_sum(1)
    y_then_x(0, 1)
    y_then_x(0, 3)
    y_then_x(1, 2)
    y_then_x(1, 1)
    y_then_x(1, 3)
    y_finish(0)
    x_finish(0)
    y_finish(1)
    x_finish(1)
    near_all.wait_send()
    far_all.wait_send()
    stat_all.wait_send()
    for copy in messages + rs_list:
        copy.wait_send()


def shards(embeddings, partner, inv_temp):
    f32, bf16 = jnp.float32, jnp.bfloat16
    vmem = pl.BlockSpec(memory_space=pltpu.VMEM)
    unit = FORTH + FORTH // 2
    loss, grad = pl.pallas_call(
        kernel,
        out_shape=(jax.ShapeDtypeStruct((1, ROWS), f32), jax.ShapeDtypeStruct((192, ROWS), f32)),
        in_specs=[pl.BlockSpec(memory_space=pltpu.SMEM), vmem, pl.BlockSpec(memory_space=pltpu.HBM)],
        out_specs=(vmem, vmem),
        scratch_shapes=[
            pltpu.VMEM((ROWS, FEATS), f32),
            pltpu.VMEM((ROWS, FEATS), bf16),
            pltpu.VMEM((ROWS, 128), f32),
            pltpu.VMEM((KEYS, FEATS), bf16),
            pltpu.VMEM((ROWS, KEYS), f32),
            pltpu.VMEM((ROWS, KEYS), f32),
            pltpu.VMEM((ROWS, KEYS), bf16),
            pltpu.VMEM((ROWS, 128), f32),
            pltpu.VMEM((ROWS, 128), f32),
            pltpu.VMEM((ROWS, 128), f32),
            pltpu.VMEM((ROWS, 128), f32),
            pltpu.VMEM((2, ROWS), f32),
            pltpu.VMEM((8, 2, ROWS), f32),
            pltpu.VMEM((16, 128), f32),
            pltpu.VMEM((5, 16, 128), f32),
            pltpu.VMEM((16, 128), f32),
            pltpu.VMEM((8, 16, 128), f32),
            pltpu.VMEM((16, 128), f32),
            pltpu.VMEM((2, 2, FORTH // 2, QUART), bf16),
            pltpu.VMEM((2, 4, FORTH // 2, QUART), bf16),
            pltpu.VMEM((2, 2, FORTH // 2, QUART), bf16),
            pltpu.VMEM((2, 4, FORTH // 2, QUART), bf16),
            pltpu.VMEM((2, 2, FORTH // 2, QUART), f32),
            pltpu.VMEM((2, FORTH, QUART), f32),
            pltpu.VMEM((2, 4, FORTH, 128), f32),
            pltpu.VMEM((2, 4, FORTH, 128), f32),
            pltpu.VMEM((2, 4, unit, 128), bf16),
            pltpu.VMEM((2, 4, unit, 128), bf16),
            pltpu.VMEM((2, unit, 128), bf16),
            pltpu.VMEM((2, unit, 128), bf16),
            pltpu.VMEM((2, 4, unit, 128), bf16),
            pltpu.VMEM((2, 4, unit, 128), bf16),
            pltpu.SemaphoreType.DMA((4,)),
            pltpu.SemaphoreType.DMA((76,)),
            pltpu.SemaphoreType.DMA((76,)),
            pltpu.SemaphoreType.DMA((2,)),
            pltpu.SemaphoreType.DMA((4,)),
            pltpu.SemaphoreType.DMA((28,)),
            pltpu.SemaphoreType.DMA((28,)),
        ],
        compiler_params=pltpu.CompilerParams(
            collective_id=0, has_side_effects=True, vmem_limit_bytes=53 * 1024 * 1024
        ),
    )(inv_temp, partner.reshape(1, ROWS), embeddings)
    return (loss.reshape(ROWS), grad.T)


def solution(mesh):
    in_specs = (P("blk", None), P("blk"), P())
    out_specs = (P("blk"), P("blk", "grp"))
    return jax.shard_map(shards, mesh=mesh, in_specs=in_specs, out_specs=out_specs, check_vma=False)
```

```python
import jax
import jax.numpy as jnp
from jax import lax
from jax.experimental import pallas as pl
from jax.experimental.pallas import tpu as pltpu
from jax.sharding import PartitionSpec as P

MESH = pl.DeviceIdType.MESH
ROWS = 512
FEATS = 1536
SUB = 16
CHUNK = 256
KEYS = 2048
QUART = 384
HALF = 256
FORTH = 128
ORDER = (0, 2, 1, 3)


def tile_of(dist, side, other_y):
    if dist in (0, 4):
        return (0 if dist == 0 else 14) + other_y
    return 2 * (2 * dist - 1 + other_y) + side


TILES = {}
for _d in range(5):
    for _s in (0, 1):
        for _o in (0, 1):
            if not (_d in (0, 4) and _s == 1):
                TILES[tile_of(_d, _s, _o)] = (_d, _s, _o)


def slot(dist, side, other_y, other_core, piece):
    return 128 * tile_of(dist, side, other_y) + 64 * other_core + SUB * piece


def turn(v):
    return pltpu.roll(v, 64, axis=1)


def pack(v, mask):
    n = v.shape[0] // 2
    return jnp.where(mask, v[:n], turn(v[n:]))


def unpack(m):
    return jnp.concatenate([m, turn(m)], axis=0)


def kernel(
    temp_ref, partner_ref, emb_hbm, loss_ref, grad_ref,
    emb, query, rinv, keys, scores, expon, weights, sum_acc, pos_acc, row_inv, mate_col,
    stat_out, stat_in, col_out, col_near, col_sum, col_far, key_tot,
    far_buf, near_buf, relay_in, side_in, hold_x, acc, hold_full, hold_half,
    yo_buf, yi_buf, cross_out, cross_in, xo_buf, xi_buf,
    load_sem, ag_send, ag_recv, stat_sem, col_sem, rs_recv,
):
    blk = lax.axis_index("blk")
    grp = lax.axis_index("grp")
    ylo = lax.div(blk, 16)
    z = lax.rem(lax.div(blk, 2), 8)
    core = lax.rem(blk, 2)
    x = lax.div(grp, 2)
    yhi = lax.rem(grp, 2)
    y = yhi * 2 + ylo
    part_a = yhi
    part_b = lax.rem(yhi + ylo, 2)

    def device(x_, y_, z_, core_):
        return (lax.rem(y_, 2) * 16 + z_ * 2 + core_, x_ * 2 + lax.div(y_, 2))

    z_right = device(x, y, lax.rem(z + 1, 8), core)
    z_left = device(x, y, lax.rem(z + 7, 8), core)
    y_a = y + 1 - 2 * ylo
    y_b = 3 - y
    dev_a = device(x, y_a, z, core)
    dev_b = device(x, y_b, z, core)
    sib = device(x, y, z, 1 - core)
    x_right = device(lax.rem(x + 1, 4), y, z, core)
    x_left = device(lax.rem(x + 3, 4), y, z, core)
    x_far = device(lax.rem(x + 2, 4), y, z, core)
    dev_cross = device(x, lax.rem(y + 2, 4), z, core)
    peers = [(blk, lax.rem(grp + r, 8)) for r in range(1, 8)]

    barrier = pltpu.get_barrier_semaphore()
    greeted = [z_right, z_left, dev_a, dev_b, sib] + peers
    for target in greeted:
        pl.semaphore_signal(barrier, inc=1, device_id=target, device_id_type=MESH)

    loads = []
    for i in range(4):
        rows = pl.ds(pl.multiple_of(lax.rem(x + i, 4) * 128, 128), 128)
        copy = pltpu.make_async_copy(emb_hbm.at[rows], emb.at[rows], load_sem.at[i])
        copy.start()
        loads.append(copy)

    temper = temp_ref[0].astype(jnp.float32)

    def unit_rows(rows):
        e = emb[rows, :]
        r = lax.rsqrt(jnp.sum(e * e, axis=1, keepdims=True) + 1e-06)
        return (e * r).astype(jnp.bfloat16), r

    def normalize(i):
        first = lax.rem(x + i, 4) * 128

        def step(j, carry):
            for k in range(4):
                rows = pl.ds(pl.multiple_of(first + j * 64 + k * SUB, SUB), SUB)
                q, r = unit_rows(rows)
                query[rows, :] = q
                rinv[rows, :] = jnp.broadcast_to(r, (SUB, 128))
            return carry

        lax.fori_loop(0, 2, step, 0)

    loads[0].wait()
    for piece in range(4):
        first = x * 128 + (part_a * 32 if piece < 2 else 64 + part_b * 32) + SUB * (piece % 2)
        q, _ = unit_rows(pl.ds(pl.multiple_of(first, SUB), SUB))
        keys[SUB * piece : SUB * (piece + 1), :] = q

    pl.semaphore_wait(barrier, len(greeted))

    def message(src, dst, rows, target, send, recv):
        return pltpu.make_async_remote_copy(
            src_ref=keys.at[pl.ds(src, rows)],
            dst_ref=keys.at[pl.ds(dst, rows)],
            send_sem=ag_send.at[send],
            recv_sem=ag_recv.at[recv],
            device_id=target,
            device_id_type=MESH,
        )

    ring, across, twin = {}, {}, {}

    def ring_sem(dist, turn_):
        return 4 * (dist - 1) + turn_

    for dist in range(1, 5):
        for turn_, piece in enumerate(ORDER):
            for side in (0, 1):
                if dist == 4 and side != piece // 2:
                    continue
                src = slot(dist - 1, 0 if dist == 1 else side, 0, 0, piece)
                dst = slot(dist, 0 if dist == 4 else side, 0, 0, piece)
                sem = ring_sem(dist, turn_ if dist < 4 else turn_ // 2)
                ring[side, dist, piece] = message(src, dst, SUB, z_right if side == 0 else z_left, 0, sem)
    for dist in range(5):
        for side in (0, 1):
            if dist in (0, 4) and side == 1:
                continue
            for piece in range(4):
                across[side, dist, piece] = message(
                    slot(dist, side, 0, 0, piece),
                    slot(dist, side, 1, 0, piece),
                    SUB,
                    dev_a if piece < 2 else dev_b,
                    0,
                    14 + dist,
                )
            for other in (0, 1):
                twin[side, dist, other] = message(
                    slot(dist, side, other, 0, 0),
                    slot(dist, side, other, 1, 0),
                    4 * SUB,
                    sib,
                    1,
                    19 + 2 * dist + other,
                )

    def wait_ring(dist, turn_):
        message(0, 0, 2 * SUB, sib, 0, ring_sem(dist, turn_)).wait_recv()

    lane = lax.broadcasted_iota(jnp.int32, (1, 128), 1)

    def tile_place(tile):
        dist, side, other = TILES[tile]
        return lax.rem(z + (8 - dist if side == 0 else dist), 8), other

    def key_ids(chunk):
        ids = []
        for tile in (2 * chunk, 2 * chunk + 1):
            zk, other = tile_place(tile)
            yk = ylo if other == 0 else 1 - ylo
            ck = jnp.where(lane < 64, core, 1 - core)
            within = jnp.where(lane % 64 < 32, part_a * 32, part_b * 32 + 64) + lane % 32
            ids.append((((yk * 8 + zk) * 2 + ck) * ROWS + x * 128 + within).astype(jnp.float32))
        return jnp.concatenate(ids, axis=1)

    def score_half(chunk, half):
        cols = slice(chunk * CHUNK, (chunk + 1) * CHUNK)
        rows = slice(half * HALF, (half + 1) * HALF)
        ids = key_ids(chunk)
        s = temper * lax.dot_general(
            query[rows, :], keys[cols, :], (((1,), (1,)), ((), ())), preferred_element_type=jnp.float32
        )
        e = jnp.exp(s - temper)
        if chunk == 0:
            own = lax.broadcasted_iota(jnp.int32, (HALF, CHUNK), 0) + (blk * ROWS + half * HALF)
            e = jnp.where(own.astype(jnp.float32) == ids, 0.0, e)
        mate = mate_col[rows, :]
        mate = jnp.concatenate([mate, mate], axis=1)
        p = jnp.where(mate == ids, s, 0.0)
        scores[rows, cols] = s
        expon[rows, cols] = e
        if chunk == 0:
            sum_acc[rows, :] = e[:, :128] + e[:, 128:]
            pos_acc[rows, :] = p[:, :128] + p[:, 128:]
        else:
            sum_acc[rows, :] += e[:, :128] + e[:, 128:]
            pos_acc[rows, :] += p[:, :128] + p[:, 128:]
        total = jnp.sum(e, axis=0, keepdims=True)
        for i in (0, 1):
            zk, other = tile_place(2 * chunk + i)
            row = pl.ds(other * 8 + zk, 1)
            part = total[:, 128 * i : 128 * (i + 1)]
            if half == 0:
                col_out[row, :] = part
            else:
                col_out[row, :] += part

    for piece in ORDER:
        for side in (0, 1):
            ring[side, 1, piece].start()
        across[0, 0, piece].start()
    twin[0, 0, 0].start()
    normalize(0)
    loads[1].wait()
    normalize(1)

    def sides(dist):
        return (0,) if dist in (0, 4) else (0, 1)

    def finish_across(dist):
        message(0, 0, 4 * SUB * len(sides(dist)), sib, 0, 14 + dist).wait_recv()
        for side in sides(dist):
            twin[side, dist, 1].start()

    def finish_twin(dist, other):
        message(0, 0, 4 * SUB * len(sides(dist)), sib, 1, 19 + 2 * dist + other).wait_recv()

    def meanwhile(dist, turn_):
        if dist == 1:
            if turn_ == 0:
                loads[2].wait()
                normalize(2)
            elif turn_ == 1:
                loads[3].wait()
                normalize(3)
                mate_row = jnp.broadcast_to(partner_ref[...].astype(jnp.float32), (128, ROWS))
                mate_col[...] = mate_row.T
            elif turn_ == 2:
                finish_across(0)
            else:
                finish_twin(0, 0)
                finish_twin(0, 1)
                score_half(0, 0)
        elif turn_ == 0:
            score_half(2 * (dist - 2), 1)
        elif turn_ == 1:
            finish_twin(dist - 1, 0)
            score_half(2 * (dist - 1) - 1, 0)
        elif turn_ == 2:
            score_half(2 * (dist - 1) - 1, 1)
            finish_across(dist - 1)
        else:
            finish_twin(dist - 1, 1)
            score_half(2 * (dist - 1), 0)

    for dist in range(1, 4):
        for turn_, piece in enumerate(ORDER):
            wait_ring(dist, turn_)
            for side in (0, 1):
                if dist < 3 or side == piece // 2:
                    ring[side, dist + 1, piece].start()
                across[side, dist, piece].start()
                if turn_ == 3:
                    twin[side, dist, 0].start()
            meanwhile(dist, turn_)
    wait_ring(4, 0)
    for piece in (0, 2):
        across[0, 4, piece].start()
    meanwhile(4, 0)
    wait_ring(4, 1)
    for piece in (1, 3):
        across[0, 4, piece].start()
    twin[0, 4, 0].start()
    meanwhile(4, 1)
    meanwhile(4, 2)
    meanwhile(4, 3)
    score_half(6, 1)
    finish_across(4)
    finish_twin(4, 0)
    finish_twin(4, 1)
    score_half(7, 0)
    score_half(7, 1)

    def small(src, dst, sems, i, target):
        return pltpu.make_async_remote_copy(
            src_ref=src, dst_ref=dst, send_sem=sems.at[i], recv_sem=sems.at[i + 1],
            device_id=target, device_id_type=MESH,
        )

    near_targets = [sib, dev_a, dev_b, device(x, y_a, z, 1 - core), device(x, y_b, z, 1 - core)]
    for i, target in reversed(list(enumerate(near_targets))):
        small(col_out, col_near.at[i], col_sem, 0, target).start()
    stat_out[0:1, :] = jnp.sum(sum_acc[...].T, axis=0, keepdims=True)
    stat_out[1:2, :] = jnp.sum(pos_acc[...].T, axis=0, keepdims=True)
    for r in range(1, 8):
        small(stat_out, stat_in.at[r], stat_sem, 0, peers[r - 1]).start()
    near_all = small(col_near, col_near, col_sem, 0, sib)
    near_all.wait_recv()
    is_a = lax.broadcasted_iota(jnp.int32, (16, 128), 1) % 64 < 32

    def flip(v):
        return jnp.concatenate([v[8:], v[:8]], axis=0)

    over_a = flip(col_near[1] + turn(col_near[3]))
    over_b = flip(col_near[2] + turn(col_near[4]))
    col_sum[...] = col_out[...] + turn(col_near[0]) + jnp.where(is_a, over_a, over_b)
    for dz in range(1, 8):
        small(col_sum, col_far.at[dz], col_sem, 2, device(x, y, lax.rem(z + dz, 8), core)).start()
    stat_all = small(stat_in.at[pl.ds(1, 7)], stat_in.at[pl.ds(1, 7)], stat_sem, 0, peers[0])
    stat_all.wait_recv()
    total = stat_out[...]
    for r in range(1, 8):
        total = total + stat_in[r]
    sums = total[0:1, :]
    inverse = 1.0 / sums
    loss_ref[...] = temper + jnp.log(sums) - total[1:2, :]
    for i in range(4):
        part = slice(128 * i, 128 * (i + 1))
        row_inv[part, :] = jnp.broadcast_to(inverse[:, part], (128, 128)).T
    far_all = small(col_far.at[pl.ds(1, 7)], col_far.at[pl.ds(1, 7)], col_sem, 2, z_right)
    far_all.wait_recv()
    col_total = col_sum[...]
    for dz in range(1, 8):
        col_total = col_total + col_far[dz]
    key_tot[...] = 1.0 / col_total

    def weigh_rows(first):
        for chunk in range(8):
            cols = slice(chunk * CHUNK, (chunk + 1) * CHUNK)
            ids = key_ids(chunk)
            inv = []
            for tile in (2 * chunk, 2 * chunk + 1):
                zk, other = tile_place(tile)
                inv.append(key_tot[pl.ds(other * 8 + zk, 1), :])
            col_inv = jnp.concatenate(inv, axis=1)

            def weigh(j, carry, cols=cols, ids=ids, col_inv=col_inv, chunk=chunk):
                rows = pl.ds(pl.multiple_of(first + j * 64, 64), 64)
                ri = row_inv[rows, :]
                mate = mate_col[rows, :]
                w = expon[rows, cols] * (jnp.concatenate([ri, ri], axis=1) + col_inv)
                w = w - jnp.where(jnp.concatenate([mate, mate], axis=1) == ids, 2.0, 0.0)
                w = w.astype(jnp.bfloat16)
                weights[rows, cols] = w
                inner = w.astype(jnp.float32) * scores[rows, cols]
                inner = inner[:, :128] + inner[:, 128:]
                if chunk == 0:
                    sum_acc[rows, :] = inner
                else:
                    sum_acc[rows, :] += inner
                return carry

            lax.fori_loop(0, FORTH // 64, weigh, 0)

        def coefs(j, carry):
            rows = pl.ds(pl.multiple_of(first + j * 64, 64), 64)
            r = rinv[rows, :]
            inner = jnp.sum(sum_acc[rows, :], axis=1, keepdims=True)
            pos_acc[rows, :] = r * r * inner
            sum_acc[rows, :] = r * temper
            return carry

        lax.fori_loop(0, FORTH // 64, coefs, 0)

    def grad_piece(ahead, first):
        cols = pl.ds(pl.multiple_of(lax.rem(x + ahead, 4) * QUART, QUART), QUART)
        rows = pl.ds(first, FORTH)
        d = jnp.dot(weights[rows, :], keys[:, cols], preferred_element_type=jnp.float32)
        u = sum_acc[rows, :]
        v = pos_acc[rows, :]
        return d * jnp.concatenate([u] * 3, axis=1) - emb[rows, cols] * jnp.concatenate([v] * 3, axis=1)

    def rs_message(src, dst, target, i):
        return pltpu.make_async_remote_copy(
            src_ref=src, dst_ref=dst, send_sem=ag_send.at[2], recv_sem=rs_recv.at[i],
            device_id=target, device_id_type=MESH,
        )

    def rs_wait(i, copies):
        part = keys.at[pl.ds(0, SUB * copies)]
        rs_message(part, part, x_right, i).wait_recv()

    lane_high = lane >= 64
    mine = lane_high == (yhi == 1)
    other = lane_high == (yhi == 0)
    f32, bf16 = jnp.float32, jnp.bfloat16

    def my_full(t0, t2):
        return jnp.where(yhi == 0, t0, t2)

    def write(first, full, half):
        rows = slice(first, first + FORTH)
        full, half = full.T, half.T
        grad_ref[0:64, rows] = jnp.where(yhi == 0, full[:64], half[64:])
        grad_ref[64:128, rows] = jnp.where(yhi == 0, full[64:], full[:64])
        grad_ref[128:192, rows] = jnp.where(yhi == 0, half[:64], full[64:])

    top, bot = slice(0, FORTH // 2), slice(FORTH // 2, FORTH)
    far_right, far_left, right_bot, left_top, right_top, left_bot, cross = ([] for _ in range(7))
    for q in (0, 1):
        far_right.append(rs_message(far_buf.at[q, 0], relay_in.at[q, 0], x_right, q))
        far_left.append(rs_message(far_buf.at[q, 1], relay_in.at[q, 1], x_left, q))
        right_bot.append(rs_message(near_buf.at[q, 0], side_in.at[q, 0], x_right, 2 + q))
        left_top.append(rs_message(near_buf.at[q, 1], side_in.at[q, 1], x_left, 2 + q))
        right_top.append(rs_message(near_buf.at[q, 2], side_in.at[q, 2], x_right, 2 + q))
        left_bot.append(rs_message(near_buf.at[q, 3], side_in.at[q, 3], x_left, 2 + q))
        cross.append(rs_message(cross_out.at[q], cross_in.at[q], dev_cross, 4 + q))

    def x_far_parts(q):
        d = grad_piece(2, FORTH * q)
        far_buf[q, 0] = d[top].astype(bf16)
        far_right[q].start()
        far_buf[q, 1] = d[bot].astype(bf16)
        far_left[q].start()

    def x_near_parts(q):
        d = grad_piece(1, FORTH * q)
        near_buf[q, 0] = d[bot].astype(bf16)
        right_bot[q].start()
        hold_x[q, 0] = d[top]
        d = grad_piece(3, FORTH * q)
        near_buf[q, 1] = d[top].astype(bf16)
        left_top[q].start()
        hold_x[q, 1] = d[bot]

    def x_relay(q):
        rs_wait(q, 2)
        near_buf[q, 2] = (hold_x[q, 0] + relay_in[q, 0].astype(f32)).astype(bf16)
        right_top[q].start()
        near_buf[q, 3] = (hold_x[q, 1] + relay_in[q, 1].astype(f32)).astype(bf16)
        left_bot[q].start()

    def x_own(q):
        acc[q] = grad_piece(0, FORTH * q)

    def x_sum(q):
        rs_wait(2 + q, 4)
        high = acc[q, top, :] + side_in[q, 1].astype(f32) + side_in[q, 2].astype(f32)
        low = acc[q, bot, :] + side_in[q, 0].astype(f32) + side_in[q, 3].astype(f32)
        d = jnp.concatenate([high, low], axis=0)
        t0, t1, t2 = d[:, :128], d[:, 128:256], d[:, 256:]
        cross_out[q, 0:FORTH, :] = my_full(t2, t0).astype(bf16)
        cross_out[q, FORTH:, :] = pack(t1, other).astype(bf16)
        cross[q].start()
        acc[q, :, 0:128] = my_full(t0, t2)
        acc[q, :, 128:256] = t1

    def x_finish(q):
        cross[q].wait_recv()
        full = acc[q, :, 0:128] + cross_in[q, 0:FORTH, :].astype(f32)
        half = acc[q, :, 128:256] + unpack(cross_in[q, FORTH:, :].astype(f32))
        write(FORTH * q, full, half)

    y_first = [[rs_message(yo_buf.at[q, a], yi_buf.at[q, a], dev_cross, 6 + 4 * q + a) for a in range(4)] for q in (0, 1)]
    to = {1: x_right, 2: x_far, 3: x_left}
    x_second = [{a: rs_message(xo_buf.at[q, a], xi_buf.at[q, a], to[a], 14 + q) for a in (1, 2, 3)} for q in (0, 1)]

    def y_send(q, a):
        d = grad_piece(a, HALF + FORTH * q)
        t0, t1, t2 = d[:, :128], d[:, 128:256], d[:, 256:]
        yo_buf[q, a, 0:FORTH, :] = my_full(t2, t0).astype(bf16)
        yo_buf[q, a, FORTH:, :] = pack(t1, other).astype(bf16)
        y_first[q][a].start()
        hold_full[q, a] = my_full(t0, t2)
        hold_half[q, a] = t1

    def y_add(q, a):
        y_first[q][a].wait_recv()
        full = hold_full[q, a] + yi_buf[q, a, 0:FORTH, :].astype(f32)
        half = hold_half[q, a] + unpack(yi_buf[q, a, FORTH:, :].astype(f32))
        return full, half

    def y_then_x(q, a):
        full, half = y_add(q, a)
        xo_buf[q, a, 0:FORTH, :] = full.astype(bf16)
        xo_buf[q, a, FORTH:, :] = pack(half, mine).astype(bf16)
        x_second[q][a].start()

    def y_finish(q):
        full, half = y_add(q, 0)
        rs_wait(14 + q, 3)
        for a in (2, 1, 3):
            full = full + xi_buf[q, a, 0:FORTH, :].astype(f32)
            half = half + unpack(xi_buf[q, a, FORTH:, :].astype(f32))
        write(HALF + FORTH * q, full, half)

    weigh_rows(0)
    x_far_parts(0)
    weigh_rows(HALF)
    y_send(0, 2)
    y_send(0, 1)
    weigh_rows(FORTH)
    x_far_parts(1)
    x_near_parts(0)
    y_send(0, 3)
    x_relay(0)
    weigh_rows(HALF + FORTH)
    y_send(1, 2)
    x_near_parts(1)
    x_relay(1)
    y_send(1, 1)
    y_send(1, 3)
    y_send(0, 0)
    y_send(1, 0)
    x_own(0)
    x_sum(0)
    y_then_x(0, 2)
    x_own(1)
    x_sum(1)
    y_then_x(0, 1)
    y_then_x(0, 3)
    y_then_x(1, 2)
    y_then_x(1, 1)
    y_then_x(1, 3)
    y_finish(0)
    x_finish(0)
    y_finish(1)
    x_finish(1)
    near_all.wait_send()
    far_all.wait_send()
    stat_all.wait_send()
    for send, rows in ((0, 60 * SUB), (1, 64 * SUB), (2, 28 * SUB)):
        message(0, 0, rows, sib, send, 0).wait_send()


def shards(embeddings, partner, inv_temp):
    f32, bf16 = jnp.float32, jnp.bfloat16
    vmem = pl.BlockSpec(memory_space=pltpu.VMEM)
    unit = FORTH + FORTH // 2
    loss, grad = pl.pallas_call(
        kernel,
        out_shape=(jax.ShapeDtypeStruct((1, ROWS), f32), jax.ShapeDtypeStruct((192, ROWS), f32)),
        in_specs=[pl.BlockSpec(memory_space=pltpu.SMEM), vmem, pl.BlockSpec(memory_space=pltpu.HBM)],
        out_specs=(vmem, vmem),
        scratch_shapes=[
            pltpu.VMEM((ROWS, FEATS), f32),
            pltpu.VMEM((ROWS, FEATS), bf16),
            pltpu.VMEM((ROWS, 128), f32),
            pltpu.VMEM((KEYS, FEATS), bf16),
            pltpu.VMEM((ROWS, KEYS), f32),
            pltpu.VMEM((ROWS, KEYS), f32),
            pltpu.VMEM((ROWS, KEYS), bf16),
            pltpu.VMEM((ROWS, 128), f32),
            pltpu.VMEM((ROWS, 128), f32),
            pltpu.VMEM((ROWS, 128), f32),
            pltpu.VMEM((ROWS, 128), f32),
            pltpu.VMEM((2, ROWS), f32),
            pltpu.VMEM((8, 2, ROWS), f32),
            pltpu.VMEM((16, 128), f32),
            pltpu.VMEM((5, 16, 128), f32),
            pltpu.VMEM((16, 128), f32),
            pltpu.VMEM((8, 16, 128), f32),
            pltpu.VMEM((16, 128), f32),
            pltpu.VMEM((2, 2, FORTH // 2, QUART), bf16),
            pltpu.VMEM((2, 4, FORTH // 2, QUART), bf16),
            pltpu.VMEM((2, 2, FORTH // 2, QUART), bf16),
            pltpu.VMEM((2, 4, FORTH // 2, QUART), bf16),
            pltpu.VMEM((2, 2, FORTH // 2, QUART), f32),
            pltpu.VMEM((2, FORTH, QUART), f32),
            pltpu.VMEM((2, 4, FORTH, 128), f32),
            pltpu.VMEM((2, 4, FORTH, 128), f32),
            pltpu.VMEM((2, 4, unit, 128), bf16),
            pltpu.VMEM((2, 4, unit, 128), bf16),
            pltpu.VMEM((2, unit, 128), bf16),
            pltpu.VMEM((2, unit, 128), bf16),
            pltpu.VMEM((2, 4, unit, 128), bf16),
            pltpu.VMEM((2, 4, unit, 128), bf16),
            pltpu.SemaphoreType.DMA((4,)),
            pltpu.SemaphoreType.DMA((3,)),
            pltpu.SemaphoreType.DMA((29,)),
            pltpu.SemaphoreType.DMA((2,)),
            pltpu.SemaphoreType.DMA((4,)),
            pltpu.SemaphoreType.DMA((16,)),
        ],
        compiler_params=pltpu.CompilerParams(
            collective_id=0, has_side_effects=True, vmem_limit_bytes=53 * 1024 * 1024
        ),
    )(inv_temp, partner.reshape(1, ROWS), embeddings)
    return (loss.reshape(ROWS), grad.T)


def solution(mesh):
    in_specs = (P("blk", None), P("blk"), P())
    out_specs = (P("blk"), P("blk", "grp"))
    return jax.shard_map(shards, mesh=mesh, in_specs=in_specs, out_specs=out_specs, check_vma=False)
```

```python
import jax
import jax.numpy as jnp
from jax import lax
from jax.experimental import pallas as pl
from jax.experimental.pallas import tpu as pltpu
from jax.sharding import PartitionSpec as P

MESH = pl.DeviceIdType.MESH
ROWS = 512
FEATS = 1536
SUB = 16
CHUNK = 256
KEYS = 2048
QUART = 384
HALF = 256
FORTH = 128
ORDER = (0, 2, 1, 3)


def tile_of(dist, side, other_y):
    if dist in (0, 4):
        return (0 if dist == 0 else 14) + other_y
    return 2 * (2 * dist - 1 + other_y) + side


TILES = {}
for _d in range(5):
    for _s in (0, 1):
        for _o in (0, 1):
            if not (_d in (0, 4) and _s == 1):
                TILES[tile_of(_d, _s, _o)] = (_d, _s, _o)


def slot(dist, side, other_y, other_core, piece):
    return 128 * tile_of(dist, side, other_y) + 64 * other_core + SUB * piece


def turn(v):
    return pltpu.roll(v, 64, axis=1)


def pack(v, mask):
    n = v.shape[0] // 2
    return jnp.where(mask, v[:n], turn(v[n:]))


def unpack(m):
    return jnp.concatenate([m, turn(m)], axis=0)


def kernel(
    temp_ref, partner_ref, emb_hbm, loss_ref, grad_ref,
    emb, query, rinv, keys, scores, expon, weights, sum_acc, pos_acc, row_inv, mate_col,
    stat_out, stat_in, col_out, col_near, col_sum, col_far, key_tot,
    far_buf, near_buf, relay_in, side_in, hold_x, acc, hold_full, hold_half,
    yo_buf, yi_buf, cross_out, cross_in, xo_buf, xi_buf,
    load_sem, ag_send, ag_recv, stat_sem, col_sem, rs_recv,
):
    blk = lax.axis_index("blk")
    grp = lax.axis_index("grp")
    ylo = lax.div(blk, 16)
    z = lax.rem(lax.div(blk, 2), 8)
    core = lax.rem(blk, 2)
    x = lax.div(grp, 2)
    yhi = lax.rem(grp, 2)
    y = yhi * 2 + ylo
    part_a = yhi
    part_b = lax.rem(yhi + ylo, 2)

    def device(x_, y_, z_, core_):
        return (lax.rem(y_, 2) * 16 + z_ * 2 + core_, x_ * 2 + lax.div(y_, 2))

    z_right = device(x, y, lax.rem(z + 1, 8), core)
    z_left = device(x, y, lax.rem(z + 7, 8), core)
    y_a = y + 1 - 2 * ylo
    y_b = 3 - y
    dev_a = device(x, y_a, z, core)
    dev_b = device(x, y_b, z, core)
    sib = device(x, y, z, 1 - core)
    x_right = device(lax.rem(x + 1, 4), y, z, core)
    x_left = device(lax.rem(x + 3, 4), y, z, core)
    x_far = device(lax.rem(x + 2, 4), y, z, core)
    dev_cross = device(x, lax.rem(y + 2, 4), z, core)
    peers = [(blk, lax.rem(grp + r, 8)) for r in range(1, 8)]

    barrier = pltpu.get_barrier_semaphore()
    greeted = [z_right, z_left, dev_a, dev_b, sib] + peers
    for target in greeted:
        pl.semaphore_signal(barrier, inc=1, device_id=target, device_id_type=MESH)

    loads = []
    for i in range(4):
        rows = pl.ds(pl.multiple_of(lax.rem(x + i, 4) * 128, 128), 128)
        copy = pltpu.make_async_copy(emb_hbm.at[rows], emb.at[rows], load_sem.at[i])
        copy.start()
        loads.append(copy)

    temper = temp_ref[0].astype(jnp.float32)

    def unit_rows(rows):
        e = emb[rows, :]
        r = lax.rsqrt(jnp.sum(e * e, axis=1, keepdims=True) + 1e-06)
        return (e * r).astype(jnp.bfloat16), r

    def normalize(i):
        first = lax.rem(x + i, 4) * 128

        def step(j, carry):
            for k in range(4):
                rows = pl.ds(pl.multiple_of(first + j * 64 + k * SUB, SUB), SUB)
                q, r = unit_rows(rows)
                query[rows, :] = q
                rinv[rows, :] = jnp.broadcast_to(r, (SUB, 128))
            return carry

        lax.fori_loop(0, 2, step, 0)

    loads[0].wait()
    for piece in range(4):
        first = x * 128 + (part_a * 32 if piece < 2 else 64 + part_b * 32) + SUB * (piece % 2)
        q, _ = unit_rows(pl.ds(pl.multiple_of(first, SUB), SUB))
        keys[SUB * piece : SUB * (piece + 1), :] = q

    pl.semaphore_wait(barrier, len(greeted))

    def message(src, dst, rows, target, send, recv):
        return pltpu.make_async_remote_copy(
            src_ref=keys.at[pl.ds(src, rows)],
            dst_ref=keys.at[pl.ds(dst, rows)],
            send_sem=ag_send.at[send],
            recv_sem=ag_recv.at[recv],
            device_id=target,
            device_id_type=MESH,
        )

    ring, across, twin = {}, {}, {}

    def ring_sem(dist, turn_):
        return 4 * (dist - 1) + turn_

    for dist in range(1, 5):
        for turn_, piece in enumerate(ORDER):
            for side in (0, 1):
                if dist == 4 and side != piece // 2:
                    continue
                src = slot(dist - 1, 0 if dist == 1 else side, 0, 0, piece)
                dst = slot(dist, 0 if dist == 4 else side, 0, 0, piece)
                sem = ring_sem(dist, turn_ if dist < 4 else turn_ // 2)
                ring[side, dist, piece] = message(src, dst, SUB, z_right if side == 0 else z_left, 0, sem)
    for dist in range(5):
        for side in (0, 1):
            if dist in (0, 4) and side == 1:
                continue
            for piece in range(4):
                across[side, dist, piece] = message(
                    slot(dist, side, 0, 0, piece),
                    slot(dist, side, 1, 0, piece),
                    SUB,
                    dev_a if piece < 2 else dev_b,
                    0,
                    14 + dist,
                )
            for other in (0, 1):
                twin[side, dist, other] = message(
                    slot(dist, side, other, 0, 0),
                    slot(dist, side, other, 1, 0),
                    4 * SUB,
                    sib,
                    1,
                    19 + 2 * dist + other,
                )

    def wait_ring(dist, turn_):
        message(0, 0, 2 * SUB, sib, 0, ring_sem(dist, turn_)).wait_recv()

    lane = lax.broadcasted_iota(jnp.int32, (1, 128), 1)

    def tile_place(tile):
        dist, side, other = TILES[tile]
        return lax.rem(z + (8 - dist if side == 0 else dist), 8), other

    def tile_ids(tile):
        zk, other = tile_place(tile)
        yk = ylo if other == 0 else 1 - ylo
        ck = jnp.where(lane < 64, core, 1 - core)
        within = jnp.where(lane % 64 < 32, part_a * 32, part_b * 32 + 64) + lane % 32
        return (((yk * 8 + zk) * 2 + ck) * ROWS + x * 128 + within).astype(jnp.float32)

    def key_ids(chunk):
        return jnp.concatenate([tile_ids(2 * chunk), tile_ids(2 * chunk + 1)], axis=1)

    def score_half(chunk, half):
        cols = slice(chunk * CHUNK, (chunk + 1) * CHUNK)
        rows = slice(half * HALF, (half + 1) * HALF)
        ids = key_ids(chunk)
        s = temper * lax.dot_general(
            query[rows, :], keys[cols, :], (((1,), (1,)), ((), ())), preferred_element_type=jnp.float32
        )
        e = jnp.exp(s - temper)
        if chunk == 0:
            own = lax.broadcasted_iota(jnp.int32, (HALF, CHUNK), 0) + (blk * ROWS + half * HALF)
            e = jnp.where(own.astype(jnp.float32) == ids, 0.0, e)
        mate = mate_col[rows, :]
        mate = jnp.concatenate([mate, mate], axis=1)
        p = jnp.where(mate == ids, s, 0.0)
        scores[rows, cols] = s
        expon[rows, cols] = e
        if chunk == 0:
            sum_acc[rows, :] = e[:, :128] + e[:, 128:]
            pos_acc[rows, :] = p[:, :128] + p[:, 128:]
        else:
            sum_acc[rows, :] += e[:, :128] + e[:, 128:]
            pos_acc[rows, :] += p[:, :128] + p[:, 128:]
        total = jnp.sum(e, axis=0, keepdims=True)
        for i in (0, 1):
            zk, other = tile_place(2 * chunk + i)
            row = pl.ds(other * 8 + zk, 1)
            part = total[:, 128 * i : 128 * (i + 1)]
            if half == 0:
                col_out[row, :] = part
            else:
                col_out[row, :] += part

    for piece in ORDER:
        for side in (0, 1):
            ring[side, 1, piece].start()
        across[0, 0, piece].start()
    twin[0, 0, 0].start()
    normalize(0)
    loads[1].wait()
    normalize(1)

    def sides(dist):
        return (0,) if dist in (0, 4) else (0, 1)

    def finish_across(dist):
        message(0, 0, 4 * SUB * len(sides(dist)), sib, 0, 14 + dist).wait_recv()
        for side in sides(dist):
            twin[side, dist, 1].start()

    def finish_twin(dist, other):
        message(0, 0, 4 * SUB * len(sides(dist)), sib, 1, 19 + 2 * dist + other).wait_recv()

    def meanwhile(dist, turn_):
        if dist == 1:
            if turn_ == 0:
                loads[2].wait()
                normalize(2)
            elif turn_ == 1:
                loads[3].wait()
                normalize(3)
                mate_row = jnp.broadcast_to(partner_ref[...].astype(jnp.float32), (128, ROWS))
                mate_col[...] = mate_row.T
            elif turn_ == 2:
                finish_across(0)
            else:
                finish_twin(0, 0)
                finish_twin(0, 1)
                score_half(0, 0)
        elif turn_ == 0:
            score_half(2 * (dist - 2), 1)
        elif turn_ == 1:
            finish_twin(dist - 1, 0)
            score_half(2 * (dist - 1) - 1, 0)
        elif turn_ == 2:
            score_half(2 * (dist - 1) - 1, 1)
            finish_across(dist - 1)
        else:
            finish_twin(dist - 1, 1)
            score_half(2 * (dist - 1), 0)

    for dist in range(1, 4):
        for turn_, piece in enumerate(ORDER):
            wait_ring(dist, turn_)
            for side in (0, 1):
                if dist < 3 or side == piece // 2:
                    ring[side, dist + 1, piece].start()
                across[side, dist, piece].start()
                if turn_ == 3:
                    twin[side, dist, 0].start()
            meanwhile(dist, turn_)
    wait_ring(4, 0)
    for piece in (0, 2):
        across[0, 4, piece].start()
    meanwhile(4, 0)
    wait_ring(4, 1)
    for piece in (1, 3):
        across[0, 4, piece].start()
    twin[0, 4, 0].start()
    meanwhile(4, 1)
    meanwhile(4, 2)
    meanwhile(4, 3)
    score_half(6, 1)
    finish_across(4)
    finish_twin(4, 0)
    finish_twin(4, 1)
    score_half(7, 0)
    score_half(7, 1)

    def small(src, dst, sems, i, target):
        return pltpu.make_async_remote_copy(
            src_ref=src, dst_ref=dst, send_sem=sems.at[i], recv_sem=sems.at[i + 1],
            device_id=target, device_id_type=MESH,
        )

    near_targets = [sib, dev_a, dev_b, device(x, y_a, z, 1 - core), device(x, y_b, z, 1 - core)]
    for i, target in reversed(list(enumerate(near_targets))):
        small(col_out, col_near.at[i], col_sem, 0, target).start()
    stat_out[0:1, :] = jnp.sum(sum_acc[...].T, axis=0, keepdims=True)
    stat_out[1:2, :] = jnp.sum(pos_acc[...].T, axis=0, keepdims=True)
    for r in range(1, 8):
        small(stat_out, stat_in.at[r], stat_sem, 0, peers[r - 1]).start()
    near_all = small(col_near, col_near, col_sem, 0, sib)
    near_all.wait_recv()
    is_a = lax.broadcasted_iota(jnp.int32, (16, 128), 1) % 64 < 32

    def flip(v):
        return jnp.concatenate([v[8:], v[:8]], axis=0)

    over_a = flip(col_near[1] + turn(col_near[3]))
    over_b = flip(col_near[2] + turn(col_near[4]))
    col_sum[...] = col_out[...] + turn(col_near[0]) + jnp.where(is_a, over_a, over_b)
    for dz in range(1, 8):
        small(col_sum, col_far.at[dz], col_sem, 2, device(x, y, lax.rem(z + dz, 8), core)).start()
    stat_all = small(stat_in.at[pl.ds(1, 7)], stat_in.at[pl.ds(1, 7)], stat_sem, 0, peers[0])
    stat_all.wait_recv()
    total = stat_out[...]
    for r in range(1, 8):
        total = total + stat_in[r]
    sums = total[0:1, :]
    inverse = 1.0 / sums
    loss_ref[...] = temper + jnp.log(sums) - total[1:2, :]
    for i in range(4):
        part = slice(128 * i, 128 * (i + 1))
        row_inv[part, :] = jnp.broadcast_to(inverse[:, part], (128, 128)).T
    far_all = small(col_far.at[pl.ds(1, 7)], col_far.at[pl.ds(1, 7)], col_sem, 2, z_right)
    far_all.wait_recv()
    col_total = col_sum[...]
    for dz in range(1, 8):
        col_total = col_total + col_far[dz]
    key_tot[...] = 1.0 / col_total

    def weigh_rows(first, count=FORTH):
        for start in range(first, first + count, 32):
            rows = slice(start, start + 32)
            ri = row_inv[rows, :]
            mate = mate_col[rows, :]
            inner = jnp.zeros((32, 128), jnp.float32)
            for tile in range(16):
                cols = slice(tile * 128, (tile + 1) * 128)
                w = expon[rows, cols] * (ri + col_inv[tile])
                w = jnp.where(mate == ids[tile], w - 2.0, w)
                w = w.astype(jnp.bfloat16)
                weights[rows, cols] = w
                inner += w.astype(jnp.float32) * scores[rows, cols]
            r = rinv[rows, :]
            inner = jnp.sum(inner, axis=1, keepdims=True)
            pos_acc[rows, :] = r * r * inner
            sum_acc[rows, :] = r * temper

    ids, col_inv = [], []
    for tile in range(16):
        zk, other = tile_place(tile)
        ids.append(tile_ids(tile))
        col_inv.append(key_tot[pl.ds(other * 8 + zk, 1), :])

    def grad_piece(ahead, first, count=FORTH):
        cols = pl.ds(pl.multiple_of(lax.rem(x + ahead, 4) * QUART, QUART), QUART)
        rows = pl.ds(first, count)
        d = jnp.dot(weights[rows, :], keys[:, cols], preferred_element_type=jnp.float32)
        u = sum_acc[rows, :]
        v = pos_acc[rows, :]
        return d * jnp.concatenate([u] * 3, axis=1) - emb[rows, cols] * jnp.concatenate([v] * 3, axis=1)

    def rs_message(src, dst, target, i):
        return pltpu.make_async_remote_copy(
            src_ref=src, dst_ref=dst, send_sem=ag_send.at[2], recv_sem=rs_recv.at[i],
            device_id=target, device_id_type=MESH,
        )

    def rs_wait(i, copies):
        part = keys.at[pl.ds(0, SUB * copies)]
        rs_message(part, part, x_right, i).wait_recv()

    lane_high = lane >= 64
    mine = lane_high == (yhi == 1)
    other = lane_high == (yhi == 0)
    f32, bf16 = jnp.float32, jnp.bfloat16

    def my_full(t0, t2):
        return jnp.where(yhi == 0, t0, t2)

    def write(first, full, half):
        rows = slice(first, first + FORTH)
        full, half = full.T, half.T
        grad_ref[0:64, rows] = jnp.where(yhi == 0, full[:64], half[64:])
        grad_ref[64:128, rows] = jnp.where(yhi == 0, full[64:], full[:64])
        grad_ref[128:192, rows] = jnp.where(yhi == 0, half[:64], full[64:])

    top, bot = slice(0, FORTH // 2), slice(FORTH // 2, FORTH)
    far_right, far_left, right_bot, left_top, right_top, left_bot, cross = ([] for _ in range(7))
    for q in (0, 1):
        far_right.append(rs_message(far_buf.at[q, 0], relay_in.at[q, 0], x_right, q))
        far_left.append(rs_message(far_buf.at[q, 1], relay_in.at[q, 1], x_left, q))
        right_bot.append(rs_message(near_buf.at[q, 0], side_in.at[q, 0], x_right, 2 + q))
        left_top.append(rs_message(near_buf.at[q, 1], side_in.at[q, 1], x_left, 2 + q))
        right_top.append(rs_message(near_buf.at[q, 2], side_in.at[q, 2], x_right, 2 + q))
        left_bot.append(rs_message(near_buf.at[q, 3], side_in.at[q, 3], x_left, 2 + q))
        cross.append(rs_message(cross_out.at[q], cross_in.at[q], dev_cross, 4 + q))

    def x_far_parts(q):
        d = grad_piece(2, FORTH * q)
        far_buf[q, 0] = d[top].astype(bf16)
        far_right[q].start()
        far_buf[q, 1] = d[bot].astype(bf16)
        far_left[q].start()

    def x_near_parts(q):
        d = grad_piece(1, FORTH * q)
        near_buf[q, 0] = d[bot].astype(bf16)
        right_bot[q].start()
        hold_x[q, 0] = d[top]
        d = grad_piece(3, FORTH * q)
        near_buf[q, 1] = d[top].astype(bf16)
        left_top[q].start()
        hold_x[q, 1] = d[bot]

    def x_relay(q):
        rs_wait(q, 2)
        near_buf[q, 2] = (hold_x[q, 0] + relay_in[q, 0].astype(f32)).astype(bf16)
        right_top[q].start()
        near_buf[q, 3] = (hold_x[q, 1] + relay_in[q, 1].astype(f32)).astype(bf16)
        left_bot[q].start()

    def x_own(q):
        acc[q] = grad_piece(0, FORTH * q)

    def x_sum(q):
        rs_wait(2 + q, 4)
        high = acc[q, top, :] + side_in[q, 1].astype(f32) + side_in[q, 2].astype(f32)
        low = acc[q, bot, :] + side_in[q, 0].astype(f32) + side_in[q, 3].astype(f32)
        d = jnp.concatenate([high, low], axis=0)
        t0, t1, t2 = d[:, :128], d[:, 128:256], d[:, 256:]
        cross_out[q, 0:FORTH, :] = my_full(t2, t0).astype(bf16)
        cross_out[q, FORTH:, :] = pack(t1, other).astype(bf16)
        cross[q].start()
        acc[q, :, 0:128] = my_full(t0, t2)
        acc[q, :, 128:256] = t1

    def x_finish(q):
        cross[q].wait_recv()
        full = acc[q, :, 0:128] + cross_in[q, 0:FORTH, :].astype(f32)
        half = acc[q, :, 128:256] + unpack(cross_in[q, FORTH:, :].astype(f32))
        write(FORTH * q, full, half)

    y_first = [[rs_message(yo_buf.at[q, a], yi_buf.at[q, a], dev_cross, 6 + 4 * q + a) for a in range(4)] for q in (0, 1)]
    to = {1: x_right, 2: x_far, 3: x_left}
    x_second = [{a: rs_message(xo_buf.at[q, a], xi_buf.at[q, a], to[a], 14 + q) for a in (1, 2, 3)} for q in (0, 1)]

    def y_send(q, a):
        d = grad_piece(a, HALF + FORTH * q)
        t0, t1, t2 = d[:, :128], d[:, 128:256], d[:, 256:]
        yo_buf[q, a, 0:FORTH, :] = my_full(t2, t0).astype(bf16)
        yo_buf[q, a, FORTH:, :] = pack(t1, other).astype(bf16)
        y_first[q][a].start()
        hold_full[q, a] = my_full(t0, t2)
        hold_half[q, a] = t1

    def y_add(q, a):
        y_first[q][a].wait_recv()
        full = hold_full[q, a] + yi_buf[q, a, 0:FORTH, :].astype(f32)
        half = hold_half[q, a] + unpack(yi_buf[q, a, FORTH:, :].astype(f32))
        return full, half

    def y_then_x(q, a):
        full, half = y_add(q, a)
        xo_buf[q, a, 0:FORTH, :] = full.astype(bf16)
        xo_buf[q, a, FORTH:, :] = pack(half, mine).astype(bf16)
        x_second[q][a].start()

    def y_finish(q):
        full, half = y_add(q, 0)
        rs_wait(14 + q, 3)
        for a in (2, 1, 3):
            full = full + xi_buf[q, a, 0:FORTH, :].astype(f32)
            half = half + unpack(xi_buf[q, a, FORTH:, :].astype(f32))
        write(HALF + FORTH * q, full, half)

    weigh_rows(0)
    x_far_parts(0)
    weigh_rows(HALF)
    y_send(0, 2)
    y_send(0, 1)
    weigh_rows(FORTH)
    x_far_parts(1)
    x_near_parts(0)
    y_send(0, 3)
    x_relay(0)
    weigh_rows(HALF + FORTH)
    y_send(1, 2)
    x_near_parts(1)
    x_relay(1)
    y_send(1, 1)
    y_send(1, 3)
    y_send(0, 0)
    y_send(1, 0)
    x_own(0)
    x_sum(0)
    y_then_x(0, 2)
    x_own(1)
    x_sum(1)
    y_then_x(0, 1)
    y_then_x(0, 3)
    y_then_x(1, 2)
    y_then_x(1, 1)
    y_then_x(1, 3)
    y_finish(0)
    x_finish(0)
    y_finish(1)
    x_finish(1)
    near_all.wait_send()
    far_all.wait_send()
    stat_all.wait_send()
    for send, rows in ((0, 60 * SUB), (1, 64 * SUB), (2, 28 * SUB)):
        message(0, 0, rows, sib, send, 0).wait_send()


def shards(embeddings, partner, inv_temp):
    f32, bf16 = jnp.float32, jnp.bfloat16
    vmem = pl.BlockSpec(memory_space=pltpu.VMEM)
    unit = FORTH + FORTH // 2
    loss, grad = pl.pallas_call(
        kernel,
        out_shape=(jax.ShapeDtypeStruct((1, ROWS), f32), jax.ShapeDtypeStruct((192, ROWS), f32)),
        in_specs=[pl.BlockSpec(memory_space=pltpu.SMEM), vmem, pl.BlockSpec(memory_space=pltpu.HBM)],
        out_specs=(vmem, vmem),
        scratch_shapes=[
            pltpu.VMEM((ROWS, FEATS), f32),
            pltpu.VMEM((ROWS, FEATS), bf16),
            pltpu.VMEM((ROWS, 128), f32),
            pltpu.VMEM((KEYS, FEATS), bf16),
            pltpu.VMEM((ROWS, KEYS), f32),
            pltpu.VMEM((ROWS, KEYS), f32),
            pltpu.VMEM((ROWS, KEYS), bf16),
            pltpu.VMEM((ROWS, 128), f32),
            pltpu.VMEM((ROWS, 128), f32),
            pltpu.VMEM((ROWS, 128), f32),
            pltpu.VMEM((ROWS, 128), f32),
            pltpu.VMEM((2, ROWS), f32),
            pltpu.VMEM((8, 2, ROWS), f32),
            pltpu.VMEM((16, 128), f32),
            pltpu.VMEM((5, 16, 128), f32),
            pltpu.VMEM((16, 128), f32),
            pltpu.VMEM((8, 16, 128), f32),
            pltpu.VMEM((16, 128), f32),
            pltpu.VMEM((2, 2, FORTH // 2, QUART), bf16),
            pltpu.VMEM((2, 4, FORTH // 2, QUART), bf16),
            pltpu.VMEM((2, 2, FORTH // 2, QUART), bf16),
            pltpu.VMEM((2, 4, FORTH // 2, QUART), bf16),
            pltpu.VMEM((2, 2, FORTH // 2, QUART), f32),
            pltpu.VMEM((2, FORTH, QUART), f32),
            pltpu.VMEM((2, 4, FORTH, 128), f32),
            pltpu.VMEM((2, 4, FORTH, 128), f32),
            pltpu.VMEM((2, 4, unit, 128), bf16),
            pltpu.VMEM((2, 4, unit, 128), bf16),
            pltpu.VMEM((2, unit, 128), bf16),
            pltpu.VMEM((2, unit, 128), bf16),
            pltpu.VMEM((2, 4, unit, 128), bf16),
            pltpu.VMEM((2, 4, unit, 128), bf16),
            pltpu.SemaphoreType.DMA((4,)),
            pltpu.SemaphoreType.DMA((3,)),
            pltpu.SemaphoreType.DMA((29,)),
            pltpu.SemaphoreType.DMA((2,)),
            pltpu.SemaphoreType.DMA((4,)),
            pltpu.SemaphoreType.DMA((16,)),
        ],
        compiler_params=pltpu.CompilerParams(
            collective_id=0, has_side_effects=True, vmem_limit_bytes=53 * 1024 * 1024
        ),
    )(inv_temp, partner.reshape(1, ROWS), embeddings)
    return (loss.reshape(ROWS), grad.T)


def solution(mesh):
    in_specs = (P("blk", None), P("blk"), P())
    out_specs = (P("blk"), P("blk", "grp"))
    return jax.shard_map(shards, mesh=mesh, in_specs=in_specs, out_specs=out_specs, check_vma=False)
```

```python
import jax
import jax.numpy as jnp
from jax import lax
from jax.experimental import pallas as pl
from jax.experimental.pallas import tpu as pltpu
from jax.sharding import PartitionSpec as P

MESH = pl.DeviceIdType.MESH
ROWS = 512
FEATS = 1536
SUB = 16
CHUNK = 256
KEYS = 2048
QUART = 384
HALF = 256
FORTH = 128
ORDER = (0, 2, 1, 3)


def tile_of(dist, side, other_y):
    if dist in (0, 4):
        return (0 if dist == 0 else 14) + other_y
    return 2 * (2 * dist - 1 + other_y) + side


TILES = {}
for _d in range(5):
    for _s in (0, 1):
        for _o in (0, 1):
            if not (_d in (0, 4) and _s == 1):
                TILES[tile_of(_d, _s, _o)] = (_d, _s, _o)


def slot(dist, side, other_y, other_core, piece):
    return 128 * tile_of(dist, side, other_y) + 64 * other_core + SUB * piece


def turn(v):
    return pltpu.roll(v, 64, axis=1)


def pack(v, mask):
    n = v.shape[0] // 2
    return jnp.where(mask, v[:n], turn(v[n:]))


def unpack(m):
    return jnp.concatenate([m, turn(m)], axis=0)


def kernel(
    temp_ref, partner_ref, emb_hbm, loss_ref, grad_ref,
    emb, query, rinv, keys, scores, expon, weights, sum_acc, pos_acc, row_inv, mate_col,
    stat_out, stat_in, col_out, col_near, col_sum, col_far, key_tot,
    far_buf, near_buf, relay_in, side_in, hold_x, acc, hold_full, hold_half,
    yo_buf, yi_buf, cross_out, cross_in, xo_buf, xi_buf,
    load_sem, ag_send, ag_recv, stat_sem, col_sem, rs_recv,
):
    blk = lax.axis_index("blk")
    grp = lax.axis_index("grp")
    ylo = lax.div(blk, 16)
    z = lax.rem(lax.div(blk, 2), 8)
    core = lax.rem(blk, 2)
    x = lax.div(grp, 2)
    yhi = lax.rem(grp, 2)
    y = yhi * 2 + ylo
    part_a = yhi
    part_b = lax.rem(yhi + ylo, 2)

    def device(x_, y_, z_, core_):
        return (lax.rem(y_, 2) * 16 + z_ * 2 + core_, x_ * 2 + lax.div(y_, 2))

    z_right = device(x, y, lax.rem(z + 1, 8), core)
    z_left = device(x, y, lax.rem(z + 7, 8), core)
    y_a = y + 1 - 2 * ylo
    y_b = 3 - y
    dev_a = device(x, y_a, z, core)
    dev_b = device(x, y_b, z, core)
    sib = device(x, y, z, 1 - core)
    x_right = device(lax.rem(x + 1, 4), y, z, core)
    x_left = device(lax.rem(x + 3, 4), y, z, core)
    x_far = device(lax.rem(x + 2, 4), y, z, core)
    dev_cross = device(x, lax.rem(y + 2, 4), z, core)
    peers = [(blk, lax.rem(grp + r, 8)) for r in range(1, 8)]

    barrier = pltpu.get_barrier_semaphore()
    greeted = [z_right, z_left, dev_a, dev_b, sib] + peers
    for target in greeted:
        pl.semaphore_signal(barrier, inc=1, device_id=target, device_id_type=MESH)

    loads = []
    for i in range(4):
        rows = pl.ds(pl.multiple_of(lax.rem(x + i, 4) * 128, 128), 128)
        copy = pltpu.make_async_copy(emb_hbm.at[rows], emb.at[rows], load_sem.at[i])
        copy.start()
        loads.append(copy)

    temper = temp_ref[0].astype(jnp.float32)

    def unit_rows(rows):
        e = emb[rows, :]
        r = lax.rsqrt(jnp.sum(e * e, axis=1, keepdims=True) + 1e-06)
        return (e * r).astype(jnp.bfloat16), r

    def normalize(i):
        first = lax.rem(x + i, 4) * 128

        def step(j, carry):
            for k in range(4):
                rows = pl.ds(pl.multiple_of(first + j * 64 + k * SUB, SUB), SUB)
                q, r = unit_rows(rows)
                query[rows, :] = q
                rinv[rows, :] = jnp.broadcast_to(r, (SUB, 128))
            return carry

        lax.fori_loop(0, 2, step, 0)

    loads[0].wait()
    for piece in range(4):
        first = x * 128 + (part_a * 32 if piece < 2 else 64 + part_b * 32) + SUB * (piece % 2)
        q, _ = unit_rows(pl.ds(pl.multiple_of(first, SUB), SUB))
        keys[SUB * piece : SUB * (piece + 1), :] = q

    pl.semaphore_wait(barrier, len(greeted))

    def message(src, dst, rows, target, send, recv):
        return pltpu.make_async_remote_copy(
            src_ref=keys.at[pl.ds(src, rows)],
            dst_ref=keys.at[pl.ds(dst, rows)],
            send_sem=ag_send.at[send],
            recv_sem=ag_recv.at[recv],
            device_id=target,
            device_id_type=MESH,
        )

    ring, across, twin = {}, {}, {}

    def ring_sem(dist, turn_):
        return 4 * (dist - 1) + turn_

    for dist in range(1, 5):
        for turn_, piece in enumerate(ORDER):
            for side in (0, 1):
                if dist == 4 and side != piece // 2:
                    continue
                src = slot(dist - 1, 0 if dist == 1 else side, 0, 0, piece)
                dst = slot(dist, 0 if dist == 4 else side, 0, 0, piece)
                sem = ring_sem(dist, turn_ if dist < 4 else turn_ // 2)
                ring[side, dist, piece] = message(src, dst, SUB, z_right if side == 0 else z_left, 0, sem)
    for dist in range(5):
        for side in (0, 1):
            if dist in (0, 4) and side == 1:
                continue
            for piece in range(4):
                across[side, dist, piece] = message(
                    slot(dist, side, 0, 0, piece),
                    slot(dist, side, 1, 0, piece),
                    SUB,
                    dev_a if piece < 2 else dev_b,
                    0,
                    14 + dist,
                )
            for other in (0, 1):
                twin[side, dist, other] = message(
                    slot(dist, side, other, 0, 0),
                    slot(dist, side, other, 1, 0),
                    4 * SUB,
                    sib,
                    1,
                    19 + 2 * dist + other,
                )

    def wait_ring(dist, turn_):
        message(0, 0, 2 * SUB, sib, 0, ring_sem(dist, turn_)).wait_recv()

    lane = lax.broadcasted_iota(jnp.int32, (1, 128), 1)

    def tile_place(tile):
        dist, side, other = TILES[tile]
        return lax.rem(z + (8 - dist if side == 0 else dist), 8), other

    def tile_ids(tile):
        zk, other = tile_place(tile)
        yk = ylo if other == 0 else 1 - ylo
        ck = jnp.where(lane < 64, core, 1 - core)
        within = jnp.where(lane % 64 < 32, part_a * 32, part_b * 32 + 64) + lane % 32
        return (((yk * 8 + zk) * 2 + ck) * ROWS + x * 128 + within).astype(jnp.float32)

    def key_ids(chunk):
        return jnp.concatenate([tile_ids(2 * chunk), tile_ids(2 * chunk + 1)], axis=1)

    def score_half(chunk, half):
        cols = slice(chunk * CHUNK, (chunk + 1) * CHUNK)
        rows = slice(half * HALF, (half + 1) * HALF)
        ids = key_ids(chunk)
        s = temper * lax.dot_general(
            query[rows, :], keys[cols, :], (((1,), (1,)), ((), ())), preferred_element_type=jnp.float32
        )
        e = jnp.exp(s - temper)
        if chunk == 0:
            own = lax.broadcasted_iota(jnp.int32, (HALF, CHUNK), 0) + (blk * ROWS + half * HALF)
            e = jnp.where(own.astype(jnp.float32) == ids, 0.0, e)
        mate = mate_col[rows, :]
        mate = jnp.concatenate([mate, mate], axis=1)
        p = jnp.where(mate == ids, s, 0.0)
        scores[rows, cols] = s
        expon[rows, cols] = e
        if chunk == 0:
            sum_acc[rows, :] = e[:, :128] + e[:, 128:]
            pos_acc[rows, :] = p[:, :128] + p[:, 128:]
        else:
            sum_acc[rows, :] += e[:, :128] + e[:, 128:]
            pos_acc[rows, :] += p[:, :128] + p[:, 128:]
        total = jnp.sum(e, axis=0, keepdims=True)
        for i in (0, 1):
            zk, other = tile_place(2 * chunk + i)
            row = pl.ds(other * 8 + zk, 1)
            part = total[:, 128 * i : 128 * (i + 1)]
            if half == 0:
                col_out[row, :] = part
            else:
                col_out[row, :] += part

    for piece in ORDER:
        for side in (0, 1):
            ring[side, 1, piece].start()
        across[0, 0, piece].start()
    twin[0, 0, 0].start()
    normalize(0)
    loads[1].wait()
    normalize(1)

    def sides(dist):
        return (0,) if dist in (0, 4) else (0, 1)

    def finish_across(dist):
        message(0, 0, 4 * SUB * len(sides(dist)), sib, 0, 14 + dist).wait_recv()
        for side in sides(dist):
            twin[side, dist, 1].start()

    def finish_twin(dist, other):
        message(0, 0, 4 * SUB * len(sides(dist)), sib, 1, 19 + 2 * dist + other).wait_recv()

    def meanwhile(dist, turn_):
        if dist == 1:
            if turn_ == 0:
                loads[2].wait()
                normalize(2)
            elif turn_ == 1:
                loads[3].wait()
                normalize(3)
                mate_row = jnp.broadcast_to(partner_ref[...].astype(jnp.float32), (128, ROWS))
                mate_col[...] = mate_row.T
            elif turn_ == 2:
                finish_across(0)
            else:
                finish_twin(0, 0)
                finish_twin(0, 1)
                score_half(0, 0)
        elif turn_ == 0:
            score_half(2 * (dist - 2), 1)
        elif turn_ == 1:
            finish_twin(dist - 1, 0)
            score_half(2 * (dist - 1) - 1, 0)
        elif turn_ == 2:
            score_half(2 * (dist - 1) - 1, 1)
            finish_across(dist - 1)
        else:
            finish_twin(dist - 1, 1)
            score_half(2 * (dist - 1), 0)

    for dist in range(1, 4):
        for turn_, piece in enumerate(ORDER):
            wait_ring(dist, turn_)
            for side in (0, 1):
                if dist < 3 or side == piece // 2:
                    ring[side, dist + 1, piece].start()
                across[side, dist, piece].start()
                if turn_ == 3:
                    twin[side, dist, 0].start()
            meanwhile(dist, turn_)
    wait_ring(4, 0)
    for piece in (0, 2):
        across[0, 4, piece].start()
    meanwhile(4, 0)
    wait_ring(4, 1)
    for piece in (1, 3):
        across[0, 4, piece].start()
    twin[0, 4, 0].start()
    meanwhile(4, 1)
    meanwhile(4, 2)
    meanwhile(4, 3)
    score_half(6, 1)
    finish_across(4)
    finish_twin(4, 0)
    finish_twin(4, 1)
    score_half(7, 0)
    score_half(7, 1)

    def small(src, dst, sems, i, target):
        return pltpu.make_async_remote_copy(
            src_ref=src, dst_ref=dst, send_sem=sems.at[i], recv_sem=sems.at[i + 1],
            device_id=target, device_id_type=MESH,
        )

    near_targets = [sib, dev_a, dev_b, device(x, y_a, z, 1 - core), device(x, y_b, z, 1 - core)]
    for i, target in reversed(list(enumerate(near_targets))):
        small(col_out, col_near.at[i], col_sem, 0, target).start()
    stat_out[0:1, :] = jnp.sum(sum_acc[...].T, axis=0, keepdims=True)
    stat_out[1:2, :] = jnp.sum(pos_acc[...].T, axis=0, keepdims=True)
    for r in range(1, 8):
        small(stat_out, stat_in.at[r], stat_sem, 0, peers[r - 1]).start()
    near_all = small(col_near, col_near, col_sem, 0, sib)
    near_all.wait_recv()
    is_a = lax.broadcasted_iota(jnp.int32, (16, 128), 1) % 64 < 32

    def flip(v):
        return jnp.concatenate([v[8:], v[:8]], axis=0)

    over_a = flip(col_near[1] + turn(col_near[3]))
    over_b = flip(col_near[2] + turn(col_near[4]))
    col_sum[...] = col_out[...] + turn(col_near[0]) + jnp.where(is_a, over_a, over_b)
    for dz in range(1, 8):
        small(col_sum, col_far.at[dz], col_sem, 2, device(x, y, lax.rem(z + dz, 8), core)).start()
    stat_all = small(stat_in.at[pl.ds(1, 7)], stat_in.at[pl.ds(1, 7)], stat_sem, 0, peers[0])
    stat_all.wait_recv()
    total = stat_out[...]
    for r in range(1, 8):
        total = total + stat_in[r]
    sums = total[0:1, :]
    inverse = 1.0 / sums
    loss_ref[...] = temper + jnp.log(sums) - total[1:2, :]
    for i in range(4):
        part = slice(128 * i, 128 * (i + 1))
        row_inv[part, :] = jnp.broadcast_to(inverse[:, part], (128, 128)).T
    far_all = small(col_far.at[pl.ds(1, 7)], col_far.at[pl.ds(1, 7)], col_sem, 2, z_right)
    far_all.wait_recv()
    col_total = col_sum[...]
    for dz in range(1, 8):
        col_total = col_total + col_far[dz]
    key_tot[...] = 1.0 / col_total

    def weigh_rows(first, count=FORTH):
        for start in range(first, first + count, 32):
            rows = slice(start, start + 32)
            ri = row_inv[rows, :]
            mate = mate_col[rows, :]
            inner = jnp.zeros((32, 128), jnp.float32)
            for tile in range(16):
                cols = slice(tile * 128, (tile + 1) * 128)
                w = expon[rows, cols] * (ri + col_inv[tile])
                w = jnp.where(mate == ids[tile], w - 2.0, w)
                w = w.astype(jnp.bfloat16)
                weights[rows, cols] = w
                inner += w.astype(jnp.float32) * scores[rows, cols]
            r = rinv[rows, :]
            inner = jnp.sum(inner, axis=1, keepdims=True)
            pos_acc[rows, :] = r * r * inner
            sum_acc[rows, :] = r * temper

    ids, col_inv = [], []
    for tile in range(16):
        zk, other = tile_place(tile)
        ids.append(tile_ids(tile))
        col_inv.append(key_tot[pl.ds(other * 8 + zk, 1), :])

    def grad_piece(ahead, first, count=FORTH):
        cols = pl.ds(pl.multiple_of(lax.rem(x + ahead, 4) * QUART, QUART), QUART)
        rows = pl.ds(first, count)
        d = jnp.dot(weights[rows, :], keys[:, cols], preferred_element_type=jnp.float32)
        u = sum_acc[rows, :]
        v = pos_acc[rows, :]
        return d * jnp.concatenate([u] * 3, axis=1) - emb[rows, cols] * jnp.concatenate([v] * 3, axis=1)

    def rs_message(src, dst, target, i):
        return pltpu.make_async_remote_copy(
            src_ref=src, dst_ref=dst, send_sem=ag_send.at[2], recv_sem=rs_recv.at[i],
            device_id=target, device_id_type=MESH,
        )

    def rs_wait(i, copies):
        part = keys.at[pl.ds(0, SUB * copies)]
        rs_message(part, part, x_right, i).wait_recv()

    lane_high = lane >= 64
    mine = lane_high == (yhi == 1)
    other = lane_high == (yhi == 0)
    f32, bf16 = jnp.float32, jnp.bfloat16

    def my_full(t0, t2):
        return jnp.where(yhi == 0, t0, t2)

    def write(first, full, half):
        rows = slice(first, first + FORTH)
        full, half = full.T, half.T
        grad_ref[0:64, rows] = jnp.where(yhi == 0, full[:64], half[64:])
        grad_ref[64:128, rows] = jnp.where(yhi == 0, full[64:], full[:64])
        grad_ref[128:192, rows] = jnp.where(yhi == 0, half[:64], full[64:])

    top, bot = slice(0, FORTH // 2), slice(FORTH // 2, FORTH)
    far_right, far_left, right_bot, left_top, right_top, left_bot, cross = ([] for _ in range(7))
    for q in (0, 1):
        far_right.append(rs_message(far_buf.at[q, 0], relay_in.at[q, 0], x_right, q))
        far_left.append(rs_message(far_buf.at[q, 1], relay_in.at[q, 1], x_left, q))
        right_bot.append(rs_message(near_buf.at[q, 0], side_in.at[q, 0], x_right, 2 + q))
        left_top.append(rs_message(near_buf.at[q, 1], side_in.at[q, 1], x_left, 2 + q))
        right_top.append(rs_message(near_buf.at[q, 2], side_in.at[q, 2], x_right, 2 + q))
        left_bot.append(rs_message(near_buf.at[q, 3], side_in.at[q, 3], x_left, 2 + q))
        cross.append(rs_message(cross_out.at[q], cross_in.at[q], dev_cross, 4 + q))

    def x_far_parts(q):
        d = grad_piece(2, FORTH * q)
        far_buf[q, 0] = d[top].astype(bf16)
        far_right[q].start()
        far_buf[q, 1] = d[bot].astype(bf16)
        far_left[q].start()

    def x_near_parts(q):
        d = grad_piece(1, FORTH * q)
        near_buf[q, 0] = d[bot].astype(bf16)
        right_bot[q].start()
        hold_x[q, 0] = d[top]
        d = grad_piece(3, FORTH * q)
        near_buf[q, 1] = d[top].astype(bf16)
        left_top[q].start()
        hold_x[q, 1] = d[bot]

    def x_relay(q):
        rs_wait(q, 2)
        near_buf[q, 2] = (hold_x[q, 0] + relay_in[q, 0].astype(f32)).astype(bf16)
        right_top[q].start()
        near_buf[q, 3] = (hold_x[q, 1] + relay_in[q, 1].astype(f32)).astype(bf16)
        left_bot[q].start()

    def x_own(q):
        acc[q] = grad_piece(0, FORTH * q)

    def x_sum(q):
        rs_wait(2 + q, 4)
        high = acc[q, top, :] + side_in[q, 1].astype(f32) + side_in[q, 2].astype(f32)
        low = acc[q, bot, :] + side_in[q, 0].astype(f32) + side_in[q, 3].astype(f32)
        d = jnp.concatenate([high, low], axis=0)
        t0, t1, t2 = d[:, :128], d[:, 128:256], d[:, 256:]
        cross_out[q, 0:FORTH, :] = my_full(t2, t0).astype(bf16)
        cross_out[q, FORTH:, :] = pack(t1, other).astype(bf16)
        cross[q].start()
        acc[q, :, 0:128] = my_full(t0, t2)
        acc[q, :, 128:256] = t1

    def x_finish(q):
        cross[q].wait_recv()
        full = acc[q, :, 0:128] + cross_in[q, 0:FORTH, :].astype(f32)
        half = acc[q, :, 128:256] + unpack(cross_in[q, FORTH:, :].astype(f32))
        write(FORTH * q, full, half)

    y_first = [[rs_message(yo_buf.at[q, a], yi_buf.at[q, a], dev_cross, 6 + 4 * q + a) for a in range(4)] for q in (0, 1)]
    to = {1: x_right, 2: x_far, 3: x_left}
    x_second = [{a: rs_message(xo_buf.at[q, a], xi_buf.at[q, a], to[a], 14 + q) for a in (1, 2, 3)} for q in (0, 1)]

    def y_send(q, a):
        d = grad_piece(a, HALF + FORTH * q)
        t0, t1, t2 = d[:, :128], d[:, 128:256], d[:, 256:]
        yo_buf[q, a, 0:FORTH, :] = my_full(t2, t0).astype(bf16)
        yo_buf[q, a, FORTH:, :] = pack(t1, other).astype(bf16)
        y_first[q][a].start()
        hold_full[q, a] = my_full(t0, t2)
        hold_half[q, a] = t1

    def y_add(q, a):
        y_first[q][a].wait_recv()
        full = hold_full[q, a] + yi_buf[q, a, 0:FORTH, :].astype(f32)
        half = hold_half[q, a] + unpack(yi_buf[q, a, FORTH:, :].astype(f32))
        return full, half

    def y_then_x(q, a):
        full, half = y_add(q, a)
        xo_buf[q, a, 0:FORTH, :] = full.astype(bf16)
        xo_buf[q, a, FORTH:, :] = pack(half, mine).astype(bf16)
        x_second[q][a].start()

    def y_finish(q):
        full, half = y_add(q, 0)
        rs_wait(14 + q, 3)
        for a in (2, 1, 3):
            full = full + xi_buf[q, a, 0:FORTH, :].astype(f32)
            half = half + unpack(xi_buf[q, a, FORTH:, :].astype(f32))
        write(HALF + FORTH * q, full, half)

    weigh_rows(0)
    x_far_parts(0)
    weigh_rows(HALF)
    y_send(0, 2)
    weigh_rows(FORTH)
    x_far_parts(1)
    y_send(0, 1)
    x_near_parts(0)
    weigh_rows(HALF + FORTH)
    y_send(1, 2)
    x_relay(0)
    y_send(0, 3)
    x_near_parts(1)
    y_send(1, 1)
    x_relay(1)
    y_send(1, 3)
    y_send(0, 0)
    x_own(0)
    y_send(1, 0)
    x_sum(0)
    y_then_x(0, 2)
    x_own(1)
    x_sum(1)
    y_then_x(0, 1)
    y_then_x(0, 3)
    y_then_x(1, 2)
    y_then_x(1, 1)
    y_then_x(1, 3)
    y_finish(0)
    x_finish(0)
    y_finish(1)
    x_finish(1)
    near_all.wait_send()
    far_all.wait_send()
    stat_all.wait_send()
    for send, rows in ((0, 60 * SUB), (1, 64 * SUB), (2, 28 * SUB)):
        message(0, 0, rows, sib, send, 0).wait_send()


def shards(embeddings, partner, inv_temp):
    f32, bf16 = jnp.float32, jnp.bfloat16
    vmem = pl.BlockSpec(memory_space=pltpu.VMEM)
    unit = FORTH + FORTH // 2
    loss, grad = pl.pallas_call(
        kernel,
        out_shape=(jax.ShapeDtypeStruct((1, ROWS), f32), jax.ShapeDtypeStruct((192, ROWS), f32)),
        in_specs=[pl.BlockSpec(memory_space=pltpu.SMEM), vmem, pl.BlockSpec(memory_space=pltpu.HBM)],
        out_specs=(vmem, vmem),
        scratch_shapes=[
            pltpu.VMEM((ROWS, FEATS), f32),
            pltpu.VMEM((ROWS, FEATS), bf16),
            pltpu.VMEM((ROWS, 128), f32),
            pltpu.VMEM((KEYS, FEATS), bf16),
            pltpu.VMEM((ROWS, KEYS), f32),
            pltpu.VMEM((ROWS, KEYS), f32),
            pltpu.VMEM((ROWS, KEYS), bf16),
            pltpu.VMEM((ROWS, 128), f32),
            pltpu.VMEM((ROWS, 128), f32),
            pltpu.VMEM((ROWS, 128), f32),
            pltpu.VMEM((ROWS, 128), f32),
            pltpu.VMEM((2, ROWS), f32),
            pltpu.VMEM((8, 2, ROWS), f32),
            pltpu.VMEM((16, 128), f32),
            pltpu.VMEM((5, 16, 128), f32),
            pltpu.VMEM((16, 128), f32),
            pltpu.VMEM((8, 16, 128), f32),
            pltpu.VMEM((16, 128), f32),
            pltpu.VMEM((2, 2, FORTH // 2, QUART), bf16),
            pltpu.VMEM((2, 4, FORTH // 2, QUART), bf16),
            pltpu.VMEM((2, 2, FORTH // 2, QUART), bf16),
            pltpu.VMEM((2, 4, FORTH // 2, QUART), bf16),
            pltpu.VMEM((2, 2, FORTH // 2, QUART), f32),
            pltpu.VMEM((2, FORTH, QUART), f32),
            pltpu.VMEM((2, 4, FORTH, 128), f32),
            pltpu.VMEM((2, 4, FORTH, 128), f32),
            pltpu.VMEM((2, 4, unit, 128), bf16),
            pltpu.VMEM((2, 4, unit, 128), bf16),
            pltpu.VMEM((2, unit, 128), bf16),
            pltpu.VMEM((2, unit, 128), bf16),
            pltpu.VMEM((2, 4, unit, 128), bf16),
            pltpu.VMEM((2, 4, unit, 128), bf16),
            pltpu.SemaphoreType.DMA((4,)),
            pltpu.SemaphoreType.DMA((3,)),
            pltpu.SemaphoreType.DMA((29,)),
            pltpu.SemaphoreType.DMA((2,)),
            pltpu.SemaphoreType.DMA((4,)),
            pltpu.SemaphoreType.DMA((16,)),
        ],
        compiler_params=pltpu.CompilerParams(
            collective_id=0, has_side_effects=True, vmem_limit_bytes=53 * 1024 * 1024
        ),
    )(inv_temp, partner.reshape(1, ROWS), embeddings)
    return (loss.reshape(ROWS), grad.T)


def solution(mesh):
    in_specs = (P("blk", None), P("blk"), P())
    out_specs = (P("blk"), P("blk", "grp"))
    return jax.shard_map(shards, mesh=mesh, in_specs=in_specs, out_specs=out_specs, check_vma=False)
```

```python
import jax
import jax.numpy as jnp
from jax import lax
from jax.experimental import pallas as pl
from jax.experimental.pallas import tpu as pltpu
from jax.sharding import PartitionSpec as P

MESH = pl.DeviceIdType.MESH
ROWS = 512
FEATS = 1536
SUB = 16
CHUNK = 256
KEYS = 2048
QUART = 384
HALF = 256
FORTH = 128
ORDER = (0, 2, 1, 3)


def tile_of(dist, side, other_y):
    if dist in (0, 4):
        return (0 if dist == 0 else 14) + other_y
    return 2 * (2 * dist - 1 + other_y) + side


TILES = {}
for _d in range(5):
    for _s in (0, 1):
        for _o in (0, 1):
            if not (_d in (0, 4) and _s == 1):
                TILES[tile_of(_d, _s, _o)] = (_d, _s, _o)


def slot(dist, side, other_y, other_core, piece):
    return 128 * tile_of(dist, side, other_y) + 64 * other_core + SUB * piece


def turn(v):
    return pltpu.roll(v, 64, axis=1)


def pack(v, mask):
    n = v.shape[0] // 2
    return jnp.where(mask, v[:n], turn(v[n:]))


def unpack(m):
    return jnp.concatenate([m, turn(m)], axis=0)


def kernel(
    temp_ref, partner_ref, emb_hbm, loss_ref, grad_ref,
    emb, query, rinv, keys, scores, expon, weights, sum_acc, pos_acc, row_inv, mate_col,
    stat_out, stat_in, col_out, col_near, col_sum, col_far, key_tot,
    far_buf, near_buf, relay_in, side_in, hold_x, acc, hold_full, hold_half,
    yo_buf, yi_buf, cross_out, cross_in, xo_buf, xi_buf,
    load_sem, ag_send, ag_recv, stat_sem, col_sem, rs_recv,
):
    blk = lax.axis_index("blk")
    grp = lax.axis_index("grp")
    ylo = lax.div(blk, 16)
    z = lax.rem(lax.div(blk, 2), 8)
    core = lax.rem(blk, 2)
    x = lax.div(grp, 2)
    yhi = lax.rem(grp, 2)
    y = yhi * 2 + ylo
    part_a = yhi
    part_b = lax.rem(yhi + ylo, 2)

    def device(x_, y_, z_, core_):
        return (lax.rem(y_, 2) * 16 + z_ * 2 + core_, x_ * 2 + lax.div(y_, 2))

    z_right = device(x, y, lax.rem(z + 1, 8), core)
    z_left = device(x, y, lax.rem(z + 7, 8), core)
    y_a = y + 1 - 2 * ylo
    y_b = 3 - y
    dev_a = device(x, y_a, z, core)
    dev_b = device(x, y_b, z, core)
    sib = device(x, y, z, 1 - core)
    x_right = device(lax.rem(x + 1, 4), y, z, core)
    x_left = device(lax.rem(x + 3, 4), y, z, core)
    x_far = device(lax.rem(x + 2, 4), y, z, core)
    dev_cross = device(x, lax.rem(y + 2, 4), z, core)
    peers = [(blk, lax.rem(grp + r, 8)) for r in range(1, 8)]

    barrier = pltpu.get_barrier_semaphore()
    greeted = [z_right, z_left, dev_a, dev_b, sib] + peers
    for target in greeted:
        pl.semaphore_signal(barrier, inc=1, device_id=target, device_id_type=MESH)

    loads = []
    for i in range(4):
        rows = pl.ds(pl.multiple_of(lax.rem(x + i, 4) * 128, 128), 128)
        copy = pltpu.make_async_copy(emb_hbm.at[rows], emb.at[rows], load_sem.at[i])
        copy.start()
        loads.append(copy)

    temper = temp_ref[0].astype(jnp.float32)

    def unit_rows(rows):
        e = emb[rows, :]
        r = lax.rsqrt(jnp.sum(e * e, axis=1, keepdims=True) + 1e-06)
        return (e * r).astype(jnp.bfloat16), r

    def normalize(i):
        first = lax.rem(x + i, 4) * 128

        def step(j, carry):
            for k in range(4):
                rows = pl.ds(pl.multiple_of(first + j * 64 + k * SUB, SUB), SUB)
                q, r = unit_rows(rows)
                query[rows, :] = q
                rinv[rows, :] = jnp.broadcast_to(r, (SUB, 128))
            return carry

        lax.fori_loop(0, 2, step, 0)

    loads[0].wait()
    for piece in range(4):
        first = x * 128 + (part_a * 32 if piece < 2 else 64 + part_b * 32) + SUB * (piece % 2)
        q, _ = unit_rows(pl.ds(pl.multiple_of(first, SUB), SUB))
        keys[SUB * piece : SUB * (piece + 1), :] = q

    pl.semaphore_wait(barrier, len(greeted))

    def message(src, dst, rows, target, send, recv):
        return pltpu.make_async_remote_copy(
            src_ref=keys.at[pl.ds(src, rows)],
            dst_ref=keys.at[pl.ds(dst, rows)],
            send_sem=ag_send.at[send],
            recv_sem=ag_recv.at[recv],
            device_id=target,
            device_id_type=MESH,
        )

    ring, across, twin = {}, {}, {}

    def ring_sem(dist, turn_):
        return 4 * (dist - 1) + turn_

    for dist in range(1, 5):
        for turn_, piece in enumerate(ORDER):
            for side in (0, 1):
                if dist == 4 and side != piece // 2:
                    continue
                src = slot(dist - 1, 0 if dist == 1 else side, 0, 0, piece)
                dst = slot(dist, 0 if dist == 4 else side, 0, 0, piece)
                sem = ring_sem(dist, turn_ if dist < 4 else turn_ // 2)
                ring[side, dist, piece] = message(src, dst, SUB, z_right if side == 0 else z_left, 0, sem)
    for dist in range(5):
        for side in (0, 1):
            if dist in (0, 4) and side == 1:
                continue
            for piece in range(4):
                if dist == 4:
                    across[side, dist, piece] = message(
                        slot(3, piece // 2, 1, 0, piece),
                        slot(4, 0, 1, 0, piece),
                        SUB,
                        z_right if piece < 2 else z_left,
                        0,
                        18,
                    )
                    continue
                across[side, dist, piece] = message(
                    slot(dist, side, 0, 0, piece),
                    slot(dist, side, 1, 0, piece),
                    SUB,
                    dev_a if piece < 2 else dev_b,
                    0,
                    14 + dist,
                )
            for other in (0, 1):
                twin[side, dist, other] = message(
                    slot(dist, side, other, 0, 0),
                    slot(dist, side, other, 1, 0),
                    4 * SUB,
                    sib,
                    1,
                    19 + 2 * dist + other,
                )

    def wait_ring(dist, turn_):
        message(0, 0, 2 * SUB, sib, 0, ring_sem(dist, turn_)).wait_recv()

    lane = lax.broadcasted_iota(jnp.int32, (1, 128), 1)

    def tile_place(tile):
        dist, side, other = TILES[tile]
        return lax.rem(z + (8 - dist if side == 0 else dist), 8), other

    def tile_ids(tile):
        zk, other = tile_place(tile)
        yk = ylo if other == 0 else 1 - ylo
        ck = jnp.where(lane < 64, core, 1 - core)
        within = jnp.where(lane % 64 < 32, part_a * 32, part_b * 32 + 64) + lane % 32
        return (((yk * 8 + zk) * 2 + ck) * ROWS + x * 128 + within).astype(jnp.float32)

    def key_ids(chunk):
        return jnp.concatenate([tile_ids(2 * chunk), tile_ids(2 * chunk + 1)], axis=1)

    def score_half(chunk, half):
        cols = slice(chunk * CHUNK, (chunk + 1) * CHUNK)
        rows = slice(half * HALF, (half + 1) * HALF)
        ids = key_ids(chunk)
        s = temper * lax.dot_general(
            query[rows, :], keys[cols, :], (((1,), (1,)), ((), ())), preferred_element_type=jnp.float32
        )
        e = jnp.exp(s - temper)
        if chunk == 0:
            own = lax.broadcasted_iota(jnp.int32, (HALF, CHUNK), 0) + (blk * ROWS + half * HALF)
            e = jnp.where(own.astype(jnp.float32) == ids, 0.0, e)
        mate = mate_col[rows, :]
        mate = jnp.concatenate([mate, mate], axis=1)
        p = jnp.where(mate == ids, s, 0.0)
        scores[rows, cols] = s
        expon[rows, cols] = e
        if chunk == 0:
            sum_acc[rows, :] = e[:, :128] + e[:, 128:]
            pos_acc[rows, :] = p[:, :128] + p[:, 128:]
        else:
            sum_acc[rows, :] += e[:, :128] + e[:, 128:]
            pos_acc[rows, :] += p[:, :128] + p[:, 128:]
        total = jnp.sum(e, axis=0, keepdims=True)
        for i in (0, 1):
            zk, other = tile_place(2 * chunk + i)
            row = pl.ds(other * 8 + zk, 1)
            part = total[:, 128 * i : 128 * (i + 1)]
            if half == 0:
                col_out[row, :] = part
            else:
                col_out[row, :] += part

    for piece in ORDER:
        for side in (0, 1):
            ring[side, 1, piece].start()
        across[0, 0, piece].start()
    twin[0, 0, 0].start()
    normalize(0)
    loads[1].wait()
    normalize(1)

    def sides(dist):
        return (0,) if dist in (0, 4) else (0, 1)

    def finish_across(dist):
        message(0, 0, 4 * SUB * len(sides(dist)), sib, 0, 14 + dist).wait_recv()
        for side in sides(dist):
            twin[side, dist, 1].start()

    def finish_twin(dist, other):
        message(0, 0, 4 * SUB * len(sides(dist)), sib, 1, 19 + 2 * dist + other).wait_recv()

    def meanwhile(dist, turn_):
        if dist == 1:
            if turn_ == 0:
                loads[2].wait()
                normalize(2)
            elif turn_ == 1:
                loads[3].wait()
                normalize(3)
                mate_row = jnp.broadcast_to(partner_ref[...].astype(jnp.float32), (128, ROWS))
                mate_col[...] = mate_row.T
            elif turn_ == 2:
                finish_across(0)
            else:
                finish_twin(0, 0)
                finish_twin(0, 1)
                score_half(0, 0)
        elif turn_ == 0:
            score_half(2 * (dist - 2), 1)
        elif turn_ == 1:
            finish_twin(dist - 1, 0)
            score_half(2 * (dist - 1) - 1, 0)
        elif turn_ == 2:
            score_half(2 * (dist - 1) - 1, 1)
            if dist < 4:
                finish_across(dist - 1)
        else:
            finish_twin(dist - 1, 1)
            score_half(2 * (dist - 1), 0)

    for dist in range(1, 4):
        for turn_, piece in enumerate(ORDER):
            wait_ring(dist, turn_)
            for side in (0, 1):
                if dist < 3 or side == piece // 2:
                    ring[side, dist + 1, piece].start()
                across[side, dist, piece].start()
                if turn_ == 3:
                    twin[side, dist, 0].start()
            meanwhile(dist, turn_)
    wait_ring(4, 0)
    meanwhile(4, 0)
    wait_ring(4, 1)
    twin[0, 4, 0].start()
    finish_across(3)
    for piece in ORDER:
        across[0, 4, piece].start()
    meanwhile(4, 1)
    meanwhile(4, 2)
    meanwhile(4, 3)
    score_half(6, 1)
    finish_across(4)
    finish_twin(4, 0)
    finish_twin(4, 1)
    score_half(7, 0)
    score_half(7, 1)

    def small(src, dst, sems, i, target):
        return pltpu.make_async_remote_copy(
            src_ref=src, dst_ref=dst, send_sem=sems.at[i], recv_sem=sems.at[i + 1],
            device_id=target, device_id_type=MESH,
        )

    near_targets = [sib, dev_a, dev_b, device(x, y_a, z, 1 - core), device(x, y_b, z, 1 - core)]
    for i, target in reversed(list(enumerate(near_targets))):
        small(col_out, col_near.at[i], col_sem, 0, target).start()
    stat_out[0:1, :] = jnp.sum(sum_acc[...].T, axis=0, keepdims=True)
    stat_out[1:2, :] = jnp.sum(pos_acc[...].T, axis=0, keepdims=True)
    for r in range(1, 8):
        small(stat_out, stat_in.at[r], stat_sem, 0, peers[r - 1]).start()
    near_all = small(col_near, col_near, col_sem, 0, sib)
    near_all.wait_recv()
    is_a = lax.broadcasted_iota(jnp.int32, (16, 128), 1) % 64 < 32

    def flip(v):
        return jnp.concatenate([v[8:], v[:8]], axis=0)

    over_a = flip(col_near[1] + turn(col_near[3]))
    over_b = flip(col_near[2] + turn(col_near[4]))
    col_sum[...] = col_out[...] + turn(col_near[0]) + jnp.where(is_a, over_a, over_b)
    for dz in range(1, 8):
        small(col_sum, col_far.at[dz], col_sem, 2, device(x, y, lax.rem(z + dz, 8), core)).start()
    stat_all = small(stat_in.at[pl.ds(1, 7)], stat_in.at[pl.ds(1, 7)], stat_sem, 0, peers[0])
    stat_all.wait_recv()
    total = stat_out[...]
    for r in range(1, 8):
        total = total + stat_in[r]
    sums = total[0:1, :]
    inverse = 1.0 / sums
    loss_ref[...] = temper + jnp.log(sums) - total[1:2, :]
    for i in range(4):
        part = slice(128 * i, 128 * (i + 1))
        row_inv[part, :] = jnp.broadcast_to(inverse[:, part], (128, 128)).T
    far_all = small(col_far.at[pl.ds(1, 7)], col_far.at[pl.ds(1, 7)], col_sem, 2, z_right)
    far_all.wait_recv()
    col_total = col_sum[...]
    for dz in range(1, 8):
        col_total = col_total + col_far[dz]
    key_tot[...] = 1.0 / col_total

    def weigh_rows(first, count=FORTH):
        for start in range(first, first + count, 32):
            rows = slice(start, start + 32)
            ri = row_inv[rows, :]
            mate = mate_col[rows, :]
            inner = jnp.zeros((32, 128), jnp.float32)
            for tile in range(16):
                cols = slice(tile * 128, (tile + 1) * 128)
                w = expon[rows, cols] * (ri + col_inv[tile])
                w = jnp.where(mate == ids[tile], w - 2.0, w)
                w = w.astype(jnp.bfloat16)
                weights[rows, cols] = w
                inner += w.astype(jnp.float32) * scores[rows, cols]
            r = rinv[rows, :]
            inner = jnp.sum(inner, axis=1, keepdims=True)
            pos_acc[rows, :] = r * r * inner
            sum_acc[rows, :] = r * temper

    ids, col_inv = [], []
    for tile in range(16):
        zk, other = tile_place(tile)
        ids.append(tile_ids(tile))
        col_inv.append(key_tot[pl.ds(other * 8 + zk, 1), :])

    def grad_piece(ahead, first, count=FORTH):
        cols = pl.ds(pl.multiple_of(lax.rem(x + ahead, 4) * QUART, QUART), QUART)
        rows = pl.ds(first, count)
        d = jnp.dot(weights[rows, :], keys[:, cols], preferred_element_type=jnp.float32)
        u = sum_acc[rows, :]
        v = pos_acc[rows, :]
        return d * jnp.concatenate([u] * 3, axis=1) - emb[rows, cols] * jnp.concatenate([v] * 3, axis=1)

    def rs_message(src, dst, target, i):
        return pltpu.make_async_remote_copy(
            src_ref=src, dst_ref=dst, send_sem=ag_send.at[2], recv_sem=rs_recv.at[i],
            device_id=target, device_id_type=MESH,
        )

    def rs_wait(i, copies):
        part = keys.at[pl.ds(0, SUB * copies)]
        rs_message(part, part, x_right, i).wait_recv()

    lane_high = lane >= 64
    mine = lane_high == (yhi == 1)
    other = lane_high == (yhi == 0)
    f32, bf16 = jnp.float32, jnp.bfloat16

    def my_full(t0, t2):
        return jnp.where(yhi == 0, t0, t2)

    def write(first, full, half):
        rows = slice(first, first + FORTH)
        full, half = full.T, half.T
        grad_ref[0:64, rows] = jnp.where(yhi == 0, full[:64], half[64:])
        grad_ref[64:128, rows] = jnp.where(yhi == 0, full[64:], full[:64])
        grad_ref[128:192, rows] = jnp.where(yhi == 0, half[:64], full[64:])

    top, bot = slice(0, FORTH // 2), slice(FORTH // 2, FORTH)
    far_right, far_left, right_bot, left_top, right_top, left_bot, cross = ([] for _ in range(7))
    for q in (0, 1):
        far_right.append(rs_message(far_buf.at[q, 0], relay_in.at[q, 0], x_right, q))
        far_left.append(rs_message(far_buf.at[q, 1], relay_in.at[q, 1], x_left, q))
        right_bot.append(rs_message(near_buf.at[q, 0], side_in.at[q, 0], x_right, 2 + q))
        left_top.append(rs_message(near_buf.at[q, 1], side_in.at[q, 1], x_left, 2 + q))
        right_top.append(rs_message(near_buf.at[q, 2], side_in.at[q, 2], x_right, 2 + q))
        left_bot.append(rs_message(near_buf.at[q, 3], side_in.at[q, 3], x_left, 2 + q))
        cross.append(rs_message(cross_out.at[q], cross_in.at[q], dev_cross, 4 + q))

    def x_far_parts(q):
        d = grad_piece(2, FORTH * q)
        far_buf[q, 0] = d[top].astype(bf16)
        far_right[q].start()
        far_buf[q, 1] = d[bot].astype(bf16)
        far_left[q].start()

    def x_near_parts(q):
        d = grad_piece(1, FORTH * q)
        near_buf[q, 0] = d[bot].astype(bf16)
        right_bot[q].start()
        hold_x[q, 0] = d[top]
        d = grad_piece(3, FORTH * q)
        near_buf[q, 1] = d[top].astype(bf16)
        left_top[q].start()
        hold_x[q, 1] = d[bot]

    def x_relay(q):
        rs_wait(q, 2)
        near_buf[q, 2] = (hold_x[q, 0] + relay_in[q, 0].astype(f32)).astype(bf16)
        right_top[q].start()
        near_buf[q, 3] = (hold_x[q, 1] + relay_in[q, 1].astype(f32)).astype(bf16)
        left_bot[q].start()

    def x_own(q):
        acc[q] = grad_piece(0, FORTH * q)

    def x_sum(q):
        rs_wait(2 + q, 4)
        high = acc[q, top, :] + side_in[q, 1].astype(f32) + side_in[q, 2].astype(f32)
        low = acc[q, bot, :] + side_in[q, 0].astype(f32) + side_in[q, 3].astype(f32)
        d = jnp.concatenate([high, low], axis=0)
        t0, t1, t2 = d[:, :128], d[:, 128:256], d[:, 256:]
        cross_out[q, 0:FORTH, :] = my_full(t2, t0).astype(bf16)
        cross_out[q, FORTH:, :] = pack(t1, other).astype(bf16)
        cross[q].start()
        acc[q, :, 0:128] = my_full(t0, t2)
        acc[q, :, 128:256] = t1

    def x_finish(q):
        cross[q].wait_recv()
        full = acc[q, :, 0:128] + cross_in[q, 0:FORTH, :].astype(f32)
        half = acc[q, :, 128:256] + unpack(cross_in[q, FORTH:, :].astype(f32))
        write(FORTH * q, full, half)

    y_first = [[rs_message(yo_buf.at[q, a], yi_buf.at[q, a], dev_cross, 6 + 4 * q + a) for a in range(4)] for q in (0, 1)]
    to = {1: x_right, 2: x_far, 3: x_left}
    x_second = [{a: rs_message(xo_buf.at[q, a], xi_buf.at[q, a], to[a], 14 + q) for a in (1, 2, 3)} for q in (0, 1)]

    def y_send(q, a):
        d = grad_piece(a, HALF + FORTH * q)
        t0, t1, t2 = d[:, :128], d[:, 128:256], d[:, 256:]
        yo_buf[q, a, 0:FORTH, :] = my_full(t2, t0).astype(bf16)
        yo_buf[q, a, FORTH:, :] = pack(t1, other).astype(bf16)
        y_first[q][a].start()
        hold_full[q, a] = my_full(t0, t2)
        hold_half[q, a] = t1

    def y_add(q, a):
        y_first[q][a].wait_recv()
        full = hold_full[q, a] + yi_buf[q, a, 0:FORTH, :].astype(f32)
        half = hold_half[q, a] + unpack(yi_buf[q, a, FORTH:, :].astype(f32))
        return full, half

    def y_then_x(q, a):
        full, half = y_add(q, a)
        xo_buf[q, a, 0:FORTH, :] = full.astype(bf16)
        xo_buf[q, a, FORTH:, :] = pack(half, mine).astype(bf16)
        x_second[q][a].start()

    def y_finish(q):
        full, half = y_add(q, 0)
        rs_wait(14 + q, 3)
        for a in (2, 1, 3):
            full = full + xi_buf[q, a, 0:FORTH, :].astype(f32)
            half = half + unpack(xi_buf[q, a, FORTH:, :].astype(f32))
        write(HALF + FORTH * q, full, half)

    weigh_rows(0)
    x_far_parts(0)
    weigh_rows(HALF)
    y_send(0, 2)
    weigh_rows(FORTH)
    x_far_parts(1)
    y_send(0, 1)
    x_near_parts(0)
    weigh_rows(HALF + FORTH)
    y_send(1, 2)
    x_relay(0)
    y_send(0, 3)
    x_near_parts(1)
    y_send(1, 1)
    x_relay(1)
    y_send(1, 3)
    y_send(0, 0)
    x_own(0)
    y_send(1, 0)
    x_sum(0)
    y_then_x(0, 2)
    x_own(1)
    x_sum(1)
    y_then_x(0, 1)
    y_then_x(0, 3)
    y_then_x(1, 2)
    y_then_x(1, 1)
    y_then_x(1, 3)
    y_finish(0)
    x_finish(0)
    y_finish(1)
    x_finish(1)
    near_all.wait_send()
    far_all.wait_send()
    stat_all.wait_send()
    for send, rows in ((0, 60 * SUB), (1, 64 * SUB), (2, 28 * SUB)):
        message(0, 0, rows, sib, send, 0).wait_send()


def shards(embeddings, partner, inv_temp):
    f32, bf16 = jnp.float32, jnp.bfloat16
    vmem = pl.BlockSpec(memory_space=pltpu.VMEM)
    unit = FORTH + FORTH // 2
    loss, grad = pl.pallas_call(
        kernel,
        out_shape=(jax.ShapeDtypeStruct((1, ROWS), f32), jax.ShapeDtypeStruct((192, ROWS), f32)),
        in_specs=[pl.BlockSpec(memory_space=pltpu.SMEM), vmem, pl.BlockSpec(memory_space=pltpu.HBM)],
        out_specs=(vmem, vmem),
        scratch_shapes=[
            pltpu.VMEM((ROWS, FEATS), f32),
            pltpu.VMEM((ROWS, FEATS), bf16),
            pltpu.VMEM((ROWS, 128), f32),
            pltpu.VMEM((KEYS, FEATS), bf16),
            pltpu.VMEM((ROWS, KEYS), f32),
            pltpu.VMEM((ROWS, KEYS), f32),
            pltpu.VMEM((ROWS, KEYS), bf16),
            pltpu.VMEM((ROWS, 128), f32),
            pltpu.VMEM((ROWS, 128), f32),
            pltpu.VMEM((ROWS, 128), f32),
            pltpu.VMEM((ROWS, 128), f32),
            pltpu.VMEM((2, ROWS), f32),
            pltpu.VMEM((8, 2, ROWS), f32),
            pltpu.VMEM((16, 128), f32),
            pltpu.VMEM((5, 16, 128), f32),
            pltpu.VMEM((16, 128), f32),
            pltpu.VMEM((8, 16, 128), f32),
            pltpu.VMEM((16, 128), f32),
            pltpu.VMEM((2, 2, FORTH // 2, QUART), bf16),
            pltpu.VMEM((2, 4, FORTH // 2, QUART), bf16),
            pltpu.VMEM((2, 2, FORTH // 2, QUART), bf16),
            pltpu.VMEM((2, 4, FORTH // 2, QUART), bf16),
            pltpu.VMEM((2, 2, FORTH // 2, QUART), f32),
            pltpu.VMEM((2, FORTH, QUART), f32),
            pltpu.VMEM((2, 4, FORTH, 128), f32),
            pltpu.VMEM((2, 4, FORTH, 128), f32),
            pltpu.VMEM((2, 4, unit, 128), bf16),
            pltpu.VMEM((2, 4, unit, 128), bf16),
            pltpu.VMEM((2, unit, 128), bf16),
            pltpu.VMEM((2, unit, 128), bf16),
            pltpu.VMEM((2, 4, unit, 128), bf16),
            pltpu.VMEM((2, 4, unit, 128), bf16),
            pltpu.SemaphoreType.DMA((4,)),
            pltpu.SemaphoreType.DMA((3,)),
            pltpu.SemaphoreType.DMA((29,)),
            pltpu.SemaphoreType.DMA((2,)),
            pltpu.SemaphoreType.DMA((4,)),
            pltpu.SemaphoreType.DMA((16,)),
        ],
        compiler_params=pltpu.CompilerParams(
            collective_id=0, has_side_effects=True, vmem_limit_bytes=53 * 1024 * 1024
        ),
    )(inv_temp, partner.reshape(1, ROWS), embeddings)
    return (loss.reshape(ROWS), grad.T)


def solution(mesh):
    in_specs = (P("blk", None), P("blk"), P())
    out_specs = (P("blk"), P("blk", "grp"))
    return jax.shard_map(shards, mesh=mesh, in_specs=in_specs, out_specs=out_specs, check_vma=False)
```
